128 devices in a mesh: prow: 8 (over z, core), pcol: 16 (over y, x).
Axes of the slice: x: 4, y: 4, z: 4, core: 2. Of those that a mesh axis runs over, the one named last changes fastest.
Arguments:
- matrix: float32 [20480, 20480], P('prow', 'pcol'), may hold values from -40 to 40, as said below
Outputs:
- factored: float32 [20480, 20480], P('prow', 'pcol')
The draws below stay inside these ranges and needn't reach their ends.
Inputs may be any that keep to these rules, and one draw needn't show every extreme that they name: `matrix`: A is symmetric and positive definite.
All inputs are finite; a program needn't handle non-finite values.
Results may differ from the reference program's by a relative error of at most 0.0003.
Values sent between devices are 32-bit elements; how exact they have to be, the bound alone decides.
A program may use at most 128 MiB of HBM per device.

```python
import jax
import jax.numpy as jnp
from jax import lax

NB = 256
BCOLS = 5
NBLK = 80
BROWS = 10
ORDER = 20480
N_PROW = 8
N_PCOL = 16


def draw_matrix(key, part):
    key = jax.random.fold_in(key, 11)
    first_key, second_key = jax.random.split(key, 2)
    inner = 2 * NB
    factors = jax.random.truncated_normal(first_key, -3.0, 3.0, (ORDER, inner), jnp.float32)
    gram = jnp.dot(factors, factors.T, precision=lax.Precision.HIGHEST, preferred_element_type=jnp.float32) / inner
    gram = 0.5 * (gram + gram.T)
    shift = 0.5 + jax.random.uniform(second_key, (ORDER,), jnp.float32)
    indices = jnp.arange(ORDER)
    whole = gram.at[indices, indices].add(shift)
    stored = whole.reshape(BROWS, N_PROW, NB, BCOLS, N_PCOL, NB).transpose(1, 0, 2, 4, 3, 5)
    return stored.reshape(ORDER, ORDER)


def setup_inputs(seed: int = 0) -> dict:
    key_of = jax.random.split(jax.random.key(seed), 2)
    matrix = draw_matrix(jax.random.fold_in(key_of[1], 71), 0)
    return {"matrix": matrix}


def reference(matrix):
    full_order = NB * NBLK
    blocks = jnp.arange(NBLK, dtype=jnp.int32)
    row_block = blocks % BROWS * N_PROW + blocks // BROWS
    col_block = blocks % BCOLS * N_PCOL + blocks // BCOLS
    row_global = jnp.repeat(row_block, NB)
    col_global = jnp.repeat(col_block, NB)
    within = jnp.arange(full_order, dtype=jnp.int32) % NB
    source_block = col_block % N_PROW * BROWS + col_block // N_PROW
    gather_rows = (jnp.repeat(source_block, NB) * NB + within).astype(jnp.int32)
    for panel_index in range(2):
        stored_col = panel_index % N_PCOL * BCOLS + panel_index // N_PCOL
        stored_row = panel_index % N_PROW * BROWS + panel_index // N_PROW
        column = matrix[:, stored_col * NB:(stored_col + 1) * NB]
        diagonal = column[stored_row * NB:(stored_row + 1) * NB]
        lower_factor = jnp.tril(jnp.linalg.cholesky(diagonal))
        solved = jax.scipy.linalg.solve_triangular(lower_factor, column.T, lower=True).T
        row_panel = jnp.where((row_global > panel_index)[:, None], solved, jnp.zeros_like(solved))
        row_panel = row_panel.at[stored_row * NB:(stored_row + 1) * NB].set(lower_factor)
        across = jnp.take(row_panel, gather_rows, axis=0)

        def update(element):
            piece_rows, part_panel, block_id = element
            product = lax.dot_general(part_panel.astype(jnp.float32), across.astype(jnp.float32), (((1,), (1,)), ((), ())), precision=lax.Precision.HIGHEST, preferred_element_type=jnp.float32)
            updated = piece_rows - product
            zeroed = jnp.logical_and(block_id == panel_index, (col_global > panel_index)[None, :])
            updated = jnp.where(zeroed, jnp.zeros_like(updated), updated)
            return updated.at[:, stored_col * NB:(stored_col + 1) * NB].set(part_panel)
        matrix = lax.map(update, (matrix.reshape(NBLK, NB, full_order), row_panel.reshape(NBLK, NB, NB), row_block)).reshape(full_order, full_order)
    return matrix
```

```python
import functools
import jax, jax.numpy as jnp
from jax import lax
from jax.experimental import pallas as pl
from jax.experimental.pallas import tpu as pltpu
P = jax.sharding.PartitionSpec
MESH = pl.DeviceIdType.MESH
HI = lax.Precision.HIGHEST
F32 = jnp.float32
BF16 = jnp.bfloat16
NB = 256
ROWS = 2560
COLS = 1280
CHUNK = 128
CHUNKS = ROWS // CHUNK
STRIP = 16
STRIPS = NB // STRIP
FIRST_STEP = 10
LAST_STEP = 17

def mm(a, b):
    return lax.dot_general(a, b, (((1,), (0,)), ((), ())), precision=HI, preferred_element_type=F32)

def mmt(a, b):
    return lax.dot_general(a, b, (((1,), (1,)), ((), ())), precision=HI, preferred_element_type=F32)

def full(v):
    return jnp.broadcast_to(v, (8, 128))

def leaf(w, start):
    lane = lax.broadcasted_iota(jnp.int32, (8, 128), 1)
    sub = lax.broadcasted_iota(jnp.int32, (8, 128), 0)
    other = (lane < 64) if start else (lane >= 64)
    rows = [w[8 * i:8 * i + 8, :] for i in range(8)]
    out = []
    for b in range(8):
        c = start + 8 * b
        bc = {i: [full(rows[i][:, c + k:c + k + 1]) for k in range(8)] for i in range(b, 8)}
        e = {(l, k): full(bc[b][k][l:l + 1, :]) for k in range(8) for l in range(k, 8)}
        u = [full(rows[b][k:k + 1, :]) for k in range(8)]
        done = jnp.zeros((8, 128), F32)
        for k in range(8):
            inv = 1.0 / e[k, k]
            for m in range(k + 1, 8):
                t = e[m, k] * inv
                for l in range(m, 8):
                    e[l, m] = e[l, m] - t * e[l, k]
                u[m] = u[m] - t * u[k]
                for i in range(b + 1, 8):
                    bc[i][m] = bc[i][m] - t * bc[i][k]
            scaled = u[k] * inv
            for i in range(b + 1, 8):
                rows[i] = rows[i] - bc[i][k] * scaled
            done = jnp.where(sub == k, u[k] * lax.rsqrt(e[k, k]), done)
        out.append(jnp.where(other, done, 0.0))
    return jnp.concatenate(out, axis=0)

def chol128(s):
    r = lax.broadcasted_iota(jnp.int32, (64, 128), 0)
    c = lax.broadcasted_iota(jnp.int32, (64, 128), 1)
    low = jnp.where(c == r, 1.0, 0.0)
    high = jnp.where(c == r + 64, 1.0, 0.0)
    first = leaf(jnp.where(c < 64, s[:64], high), 0)
    ma = pltpu.roll(first, 64, 1)
    l21 = mmt(jnp.where(c < 64, s[64:], 0.0), ma)
    s22 = mmt(l21, l21)
    z = jnp.zeros((64, 64), F32)
    s22 = jnp.concatenate([z, s22], axis=1)
    t = mm(l21, ma)
    second = leaf(jnp.where(c < 64, low, s[64:] - s22), 64)
    low_part = mm(second[:, :64], high - t)
    return jnp.concatenate([ma, low_part], axis=0)


PARENTS = (
    (
        (-1, 0, 3, 0, 8, 9, 10, 11, 12, 8, 14, 8, 0, 12, 15, 12),
        (1, -1, 14, 15, 5, 1, 5, 6, 9, 13, 9, 15, 13, 1, 13, 14),
    ),
    (
        (-1, 5, 6, 7, 0, 4, 7, 4, 4, 5, 11, 7, 8, 9, 10, 11),
        (3, -1, 1, 2, 7, 6, 2, 3, 11, 10, 6, 10, 15, 14, 2, 3),
    ),
)


def neighbour(chip, direction):
    y, x = chip // 4, chip % 4
    if direction < 2:
        return y * 4 + (x + (1, 3)[direction]) % 4
    return (y + (1, 3)[direction - 2]) % 4 * 4 + x


def senders(core, panel, direction):
    parents = PARENTS[core][panel]
    return [n for n in range(16) if parents[neighbour(n, direction)] == n]


MESSAGES = (
    (0, 0, 0, 0),
    (0, 1, 0, 1),
    (0, 1, 1, 2),
    (1, 0, 0, 0),
    (1, 0, 1, 1),
    (1, 1, 0, 2),
    (1, 1, 1, 0),
    (2, 0, 0, 0),
    (2, 1, 0, 1),
    (2, 1, 1, 2),
)


def panels_kernel(
    a_ref, r_ref, ct_ref, rows, slab, fac, diag, stage, lead, inv, low,
    local_sem, row_send, row_recv, slab_send, slab_recv, fac_send, fac_recv, diag_sem,
):
    prow, pcol = lax.axis_index("prow"), lax.axis_index("pcol")
    z, core = prow // 2, prow % 2
    y, x = pcol // 4, pcol % 4
    is_root = jnp.logical_and(prow == 0, pcol == 0)
    gives_diag = jnp.logical_and(prow == 1, pcol == 1)

    def device(pz, pc, py, px):
        return {"prow": pz * 2 + pc, "pcol": py * 4 + px}

    def on_line(axis, step):
        if axis == "x":
            return device(z, core, y, (x + step) % 4)
        if axis == "y":
            return device(z, core, (y + step) % 4, x)
        return device((z + step) % 4, core, y, x)

    sibling = device(z, 1 - core, y, x)

    barrier = pltpu.get_barrier_semaphore()
    for axis in "xyz":
        for step in (1, 2, 3):
            pl.semaphore_signal(barrier, 1, device_id=on_line(axis, step), device_id_type=MESH)
    pl.semaphore_signal(barrier, 1, device_id=sibling, device_id_type=MESH)

    @pl.when(is_root)
    def _():
        pl.semaphore_signal(barrier, 1, device_id={"prow": 1, "pcol": 1}, device_id_type=MESH)

    pl.semaphore_wait(barrier, 10 + jnp.where(gives_diag, 1, 0))

    index = core * 16 + pcol
    gives = [[None] * 4 for _ in range(2)]
    for k in range(2):
        for d in range(4):
            flag = jnp.int32(0)
            for c in range(2):
                for n in senders(c, k, d):
                    flag = flag + jnp.where(index == c * 16 + n, 1, 0)
            gives[k][d] = flag == 1
    targets = (on_line("x", 1), on_line("x", 3), on_line("y", 1), on_line("y", 3))

    def row_copy(src, k, d, first, count):
        piece = pl.ds(first, count)
        return pltpu.make_async_remote_copy(
            src_ref=src.at[piece, pl.ds(0, NB)] if src is a_ref else rows.at[k, piece, :],
            dst_ref=rows.at[k, piece, :],
            send_sem=row_send.at[k, d],
            recv_sem=row_recv.at[k, first // CHUNK if count == CHUNK else 0],
            device_id=targets[d],
            device_id_type=MESH,
        )

    def slab_copy(src, s, slot, first, count):
        piece = pl.ds(first, count)
        step = 1 if s == 0 else 3
        return pltpu.make_async_remote_copy(
            src_ref=a_ref.at[piece, :] if src is a_ref else slab.at[s, piece, :],
            dst_ref=slab.at[s, piece, :],
            send_sem=slab_send.at[s, slot],
            recv_sem=slab_recv.at[s, first // STRIP if count == STRIP else 0],
            device_id=on_line("z", step) if slot == 0 else sibling,
            device_id_type=MESH,
        )

    along = (
        jnp.logical_and(core == 0, z < 3),
        jnp.logical_and(core == 1, z != 1),
    )
    across = (core == 0, core == 1)

    def own_rows(k):
        return pltpu.make_async_copy(a_ref.at[:, pl.ds(0, NB)], rows.at[k], local_sem.at[k])

    def own_slab(s):
        return pltpu.make_async_copy(a_ref.at[pl.ds(0, NB), :], slab.at[s], local_sem.at[2 + s])

    def diag_copy():
        return pltpu.make_async_remote_copy(
            src_ref=a_ref.at[pl.ds(0, NB), pl.ds(0, NB)],
            dst_ref=diag,
            send_sem=diag_sem.at[0],
            recv_sem=diag_sem.at[1],
            device_id={"prow": 0, "pcol": 0},
            device_id_type=MESH,
        )

    @pl.when(gives_diag)
    def _():
        diag_copy().start()

    for s in range(2):
        @pl.when(prow == s)
        def _(s=s):
            own_slab(s).start()

    for k in range(2):
        @pl.when(pcol == k)
        def _(k=k):
            own_rows(k).start()

            def send(i, carry):
                for d in range(4):
                    @pl.when(gives[k][d])
                    def _(d=d):
                        row_copy(a_ref, k, d, i * CHUNK, CHUNK).start()
                return carry

            lax.fori_loop(0, CHUNKS, send, 0)

    for s in range(2):
        @pl.when(prow == s)
        def _(s=s):
            def send(j, carry):
                slab_copy(a_ref, s, 0, j * STRIP, STRIP).start()
                slab_copy(a_ref, s, 1, j * STRIP, STRIP).start()
                return carry

            lax.fori_loop(0, STRIPS, send, 0)

    def pass_rows(i):
        for k in range(2):
            @pl.when(pcol != k)
            def _(k=k):
                row_copy(None, k, 0, i * CHUNK, CHUNK).wait_recv()
                for d in range(4):
                    @pl.when(gives[k][d])
                    def _(d=d):
                        row_copy(None, k, d, i * CHUNK, CHUNK).start()

    def pass_slab(j):
        for s in range(2):
            @pl.when(jnp.logical_and(prow != s, jnp.logical_not(is_root)))
            def _(s=s):
                slab_copy(None, s, 0, j * STRIP, STRIP).wait_recv()

                @pl.when(along[s])
                def _():
                    slab_copy(None, s, 0, j * STRIP, STRIP).start()

                @pl.when(across[s])
                def _():
                    slab_copy(None, s, 1, j * STRIP, STRIP).start()

    where = {"x": x, "y": y, "z": z}

    def fac_targets(q):
        order = ("xyz", "yzx", "zxy")[MESSAGES[q][3]]
        at = [where[a] == 0 for a in order]
        first = jnp.logical_and(core == 0, jnp.logical_and(at[1], at[2]))
        conditions = (
            jnp.logical_and(first, at[0]),
            first,
            jnp.logical_and(core == 0, at[2]),
        )
        found = []
        for stage_index, axis in enumerate(order):
            for step in (2, 1, 3):
                found.append((conditions[stage_index], on_line(axis, step)))
        found.append((core == 0, sibling))
        return found

    def fac_copy(q, slot, target):
        m, i, j, _ = MESSAGES[q]
        piece = fac.at[m, pl.ds(i * 128, 128), pl.ds(j * 128, 128)]
        return pltpu.make_async_remote_copy(
            src_ref=piece,
            dst_ref=piece,
            send_sem=fac_send.at[q, slot],
            recv_sem=fac_recv.at[q],
            device_id=target,
            device_id_type=MESH,
        )

    def fac_start(q):
        for slot, (condition, target) in enumerate(fac_targets(q)):
            @pl.when(condition)
            def _(slot=slot, target=target):
                fac_copy(q, slot, target).start()

    def fac_pass(queue):
        @pl.when(jnp.logical_not(is_root))
        def _():
            for q in queue:
                fac_copy(q, 0, sibling).wait_recv()
                fac_start(q)

    for m in (0, 2):
        fac[m, 0:128, 128:256] = jnp.zeros((128, 128), F32)

    @pl.when(is_root)
    def _():
        own_slab(0).wait()
        stage[...] = slab[0, :, 0:NB]

        def panel(k, carry):
            lead[...] = stage[0:128, 0:128]

            def half(h, inner):
                inv[h] = chol128(lead[...])

                @pl.when(h == 0)
                def _():
                    low[...] = mmt(stage[128:256, 0:128], inv[0])
                    lead[...] = stage[128:256, 128:256] - mmt(low[...], low[...])

                return inner

            lax.fori_loop(0, 2, half, 0)
            fac[2 * k, 0:128, 0:128] = inv[0]
            fac[2 * k, 128:256, 128:256] = inv[1]
            fac[2 * k, 128:256, 0:128] = -mm(inv[1], mm(low[...], inv[0]))

            @pl.when(k == 0)
            def _():
                for q in (0, 1, 2):
                    fac_start(q)

                def arrive(j, inner):
                    slab_copy(None, 1, 0, j * STRIP, STRIP).wait_recv()
                    return inner

                lax.fori_loop(0, STRIPS, arrive, 0)
                below = mmt(slab[1, :, 0:NB], fac[0])
                fac[1] = below
                for q in (3, 4, 5, 6):
                    fac_start(q)
                diag_copy().wait_recv()
                stage[...] = diag[...] - mmt(below, below)

            @pl.when(k == 1)
            def _():
                for q in (7, 8, 9):
                    fac_start(q)

            return carry

        lax.fori_loop(0, 2, panel, 0)

    for k in range(2):
        @pl.when(pcol == k)
        def _(k=k):
            own_rows(k).wait()

    @pl.when(jnp.logical_and(prow == 0, jnp.logical_not(is_root)))
    def _():
        own_slab(0).wait()

    @pl.when(prow == 1)
    def _():
        own_slab(1).wait()

    def early(i, carry):
        pass_rows(i)
        pass_slab(i)
        return carry

    def late(i, carry):
        pass_rows(i)

        @pl.when(i < STRIPS)
        def _():
            pass_slab(i)

        block = pl.ds(pl.multiple_of((i - FIRST_STEP) * NB, NB), NB)
        first = mmt(rows[0, block, :], fac[0])
        r_ref[block, 0:NB] = first
        r_ref[block, NB:2 * NB] = rows[1, block, :] - mmt(first, fac[1])
        return carry

    lax.fori_loop(0, FIRST_STEP, early, 0)
    fac_pass((0, 1, 2, 3, 4, 5, 6))
    lax.fori_loop(FIRST_STEP, LAST_STEP, late, 0)
    fac_pass((7, 8, 9))
    lax.fori_loop(LAST_STEP, CHUNKS, late, 0)

    def columns(j, carry):
        tile = pl.ds(pl.multiple_of(j * NB, NB), NB)
        first = mm(fac[0], slab[0, :, tile])
        ct_ref[0:NB, tile] = first
        ct_ref[NB:2 * NB, tile] = mm(fac[2], slab[1, :, tile] - mm(fac[1], first))
        return carry

    lax.fori_loop(0, COLS // NB, columns, 0)

    def second(j, carry):
        block = pl.ds(pl.multiple_of(j * NB, NB), NB)
        r_ref[block, NB:2 * NB] = mmt(r_ref[block, NB:2 * NB], fac[2])
        return carry

    lax.fori_loop(0, ROWS // NB, second, 0)

    for k in range(2):
        for d in range(4):
            @pl.when(gives[k][d])
            def _(k=k, d=d):
                row_copy(None, k, d, 0, ROWS).wait_send()

    for s in range(2):
        for slot, condition in enumerate((along[s], across[s])):
            @pl.when(condition)
            def _(s=s, slot=slot):
                slab_copy(None, s, slot, 0, NB).wait_send()

    for q in range(len(MESSAGES)):
        for slot, (condition, target) in enumerate(fac_targets(q)):
            @pl.when(condition)
            def _(q=q, slot=slot, target=target):
                fac_copy(q, slot, target).wait_send()

    @pl.when(gives_diag)
    def _():
        diag_copy().wait_send()


def make_panels(matrix):
    dma = pltpu.SemaphoreType.DMA
    vmem = pl.BlockSpec(memory_space=pltpu.VMEM)
    return pl.pallas_call(
        panels_kernel,
        out_shape=(
            jax.ShapeDtypeStruct((ROWS, 2 * NB), F32),
            jax.ShapeDtypeStruct((2 * NB, COLS), F32),
        ),
        in_specs=[pl.BlockSpec(memory_space=pl.ANY)],
        out_specs=(vmem, vmem),
        scratch_shapes=[
            pltpu.VMEM((2, ROWS, NB), F32),
            pltpu.VMEM((2, NB, COLS), F32),
            pltpu.VMEM((3, NB, NB), F32),
            pltpu.VMEM((NB, NB), F32),
            pltpu.VMEM((NB, NB), F32),
            pltpu.VMEM((128, 128), F32),
            pltpu.VMEM((2, 128, 128), F32),
            pltpu.VMEM((128, 128), F32),
            dma((4,)),
            dma((2, 4)),
            dma((2, CHUNKS)),
            dma((2, 2)),
            dma((2, STRIPS)),
            dma((len(MESSAGES), 10)),
            dma((len(MESSAGES),)),
            dma((2,)),
        ],
        compiler_params=pltpu.CompilerParams(
            collective_id=0, has_side_effects=True, vmem_limit_bytes=40 * 2**20
        ),
        cost_estimate=pl.CostEstimate(
            flops=2 * 3 * ROWS * NB * NB, bytes_accessed=2**24, transcendentals=0
        ),
        name="panels",
    )(matrix)


def update_kernel(place, a_ref, r_ref, ct_ref, out_ref, c_high, c_low):
    i = pl.program_id(0)

    @pl.when(i == 0)
    def _():
        def split(j, carry):
            strip = pl.ds(pl.multiple_of(j * 64, 64), 64)
            value = ct_ref[strip, :]
            high = value.astype(BF16)
            c_high[strip, :] = high
            c_low[strip, :] = (value - high.astype(F32)).astype(BF16)
            return carry

        lax.fori_loop(0, 2 * NB // 64, split, 0)

    prow, pcol = place[0], place[1]
    row_block = i * 8 + prow
    value = r_ref[...]
    high = value.astype(BF16)
    low = (value - high.astype(F32)).astype(BF16)

    def dot(a, b):
        return lax.dot_general(a, b, (((1,), (0,)), ((), ())), preferred_element_type=F32)

    def update(j):
        tile = pl.ds(j * NB, NB)
        product = dot(high, c_high[:, tile]) + dot(high, c_low[:, tile]) + dot(low, c_high[:, tile])
        out_ref[:, tile] = a_ref[:, tile] - product

    for j in range(COLS // NB):
        tile = pl.ds(j * NB, NB)
        stays = row_block >= 2
        if j == 0:
            stays = jnp.logical_and(stays, pcol >= 2)

        @pl.when(stays)
        def _(j=j):
            update(j)

        @pl.when(jnp.logical_not(stays))
        def _(tile=tile):
            out_ref[:, tile] = jnp.zeros((NB, NB), F32)

    down = lax.broadcasted_iota(jnp.int32, (NB, NB), 0)
    right = lax.broadcasted_iota(jnp.int32, (NB, NB), 1)
    for k in range(2):
        @pl.when(jnp.logical_and(pcol == k, row_block >= k))
        def _(k=k):
            keep = jnp.logical_or(row_block > k, right <= down)
            out_ref[:, 0:NB] = jnp.where(keep, r_ref[:, k * NB:(k + 1) * NB], 0.0)


def update(matrix, row_panel, col_panel):
    place = jnp.stack([lax.axis_index("prow"), lax.axis_index("pcol")]).astype(jnp.int32)
    return pl.pallas_call(
        update_kernel,
        out_shape=jax.ShapeDtypeStruct((ROWS, COLS), F32),
        grid=(ROWS // NB,),
        in_specs=[
            pl.BlockSpec(memory_space=pltpu.SMEM),
            pl.BlockSpec((NB, COLS), lambda i: (i, 0)),
            pl.BlockSpec((NB, 2 * NB), lambda i: (i, 0)),
            pl.BlockSpec((2 * NB, COLS), lambda i: (0, 0)),
        ],
        out_specs=pl.BlockSpec((NB, COLS), lambda i: (i, 0)),
        scratch_shapes=[pltpu.VMEM((2 * NB, COLS), BF16), pltpu.VMEM((2 * NB, COLS), BF16)],
        compiler_params=pltpu.CompilerParams(vmem_limit_bytes=40 * 2**20),
        cost_estimate=pl.CostEstimate(
            flops=2 * 3 * ROWS * COLS * 2 * NB, bytes_accessed=2**25, transcendentals=0
        ),
        name="update",
    )(place, matrix, row_panel, col_panel)


def body(matrix):
    row_panel, col_panel = make_panels(matrix)
    return update(matrix, row_panel, col_panel)


def solution(mesh):
    spec = P("prow", "pcol")
    return jax.shard_map(body, mesh=mesh, in_specs=(spec,), out_specs=spec, check_vma=False)
```

```python
import functools
import jax, jax.numpy as jnp
from jax import lax
from jax.experimental import pallas as pl
from jax.experimental.pallas import tpu as pltpu
P = jax.sharding.PartitionSpec
MESH = pl.DeviceIdType.MESH
HI = lax.Precision.HIGHEST
F32 = jnp.float32
BF16 = jnp.bfloat16
NB = 256
ROWS = 2560
COLS = 1280
CHUNK = 64
CHUNKS = ROWS // CHUNK
STRIP = 16
STRIPS = NB // STRIP
LAG = 4
DEEPEST = 5
TICKS = CHUNKS + LAG * DEEPEST
FIRST_FACTOR = 18
SECOND_FACTOR = 34
COLUMNS_TICK = 35
BLOCKS_TICK = TICKS - 2 * (ROWS // NB) + 1

def mm(a, b):
    return lax.dot_general(a, b, (((1,), (0,)), ((), ())), precision=HI, preferred_element_type=F32)

def mmt(a, b):
    return lax.dot_general(a, b, (((1,), (1,)), ((), ())), precision=HI, preferred_element_type=F32)

def split(v):
    high = v.astype(BF16)
    return high, (v - high.astype(F32)).astype(BF16)


def three(a, b_high, b_low):
    def dot(p, q):
        return lax.dot_general(p, q, (((1,), (0,)), ((), ())), preferred_element_type=F32)

    high, low = split(a)
    return dot(high, b_high) + dot(high, b_low) + dot(low, b_high)


def full(v):
    return jnp.broadcast_to(v, (8, 128))

def leaf(w, start):
    lane = lax.broadcasted_iota(jnp.int32, (8, 128), 1)
    sub = lax.broadcasted_iota(jnp.int32, (8, 128), 0)
    other = (lane < 64) if start else (lane >= 64)
    rows = [w[8 * i:8 * i + 8, :] for i in range(8)]
    out = []
    for b in range(8):
        c = start + 8 * b
        bc = {i: [full(rows[i][:, c + k:c + k + 1]) for k in range(8)] for i in range(b, 8)}
        e = {(l, k): full(bc[b][k][l:l + 1, :]) for k in range(8) for l in range(k, 8)}
        u = [full(rows[b][k:k + 1, :]) for k in range(8)]
        done = jnp.zeros((8, 128), F32)
        for k in range(8):
            inv = 1.0 / e[k, k]
            for m in range(k + 1, 8):
                t = e[m, k] * inv
                for l in range(m, 8):
                    e[l, m] = e[l, m] - t * e[l, k]
                u[m] = u[m] - t * u[k]
                for i in range(b + 1, 8):
                    bc[i][m] = bc[i][m] - t * bc[i][k]
            scaled = u[k] * inv
            for i in range(b + 1, 8):
                rows[i] = rows[i] - bc[i][k] * scaled
            done = jnp.where(sub == k, u[k] * lax.rsqrt(e[k, k]), done)
        out.append(jnp.where(other, done, 0.0))
    return jnp.concatenate(out, axis=0)

def chol128(s):
    r = lax.broadcasted_iota(jnp.int32, (64, 128), 0)
    c = lax.broadcasted_iota(jnp.int32, (64, 128), 1)
    low = jnp.where(c == r, 1.0, 0.0)
    high = jnp.where(c == r + 64, 1.0, 0.0)
    first = leaf(jnp.where(c < 64, s[:64], high), 0)
    ma = pltpu.roll(first, 64, 1)
    l21 = mmt(jnp.where(c < 64, s[64:], 0.0), ma)
    s22 = mmt(l21, l21)
    z = jnp.zeros((64, 64), F32)
    s22 = jnp.concatenate([z, s22], axis=1)
    t = mm(l21, ma)
    second = leaf(jnp.where(c < 64, low, s[64:] - s22), 64)
    low_part = mm(second[:, :64], high - t)
    return jnp.concatenate([ma, low_part], axis=0)


PARENTS = (
    (
        (-1, 0, 3, 0, 8, 9, 10, 11, 12, 8, 14, 8, 0, 12, 15, 12),
        (1, -1, 14, 15, 5, 1, 5, 6, 9, 13, 9, 15, 13, 1, 13, 14),
    ),
    (
        (-1, 5, 6, 7, 0, 4, 7, 4, 4, 5, 11, 7, 8, 9, 10, 11),
        (3, -1, 1, 2, 7, 6, 2, 3, 11, 10, 6, 10, 15, 14, 2, 3),
    ),
)


def neighbour(chip, direction):
    y, x = chip // 4, chip % 4
    if direction < 2:
        return y * 4 + (x + (1, 3)[direction]) % 4
    return (y + (1, 3)[direction - 2]) % 4 * 4 + x


def depth(core, panel, chip):
    parent = PARENTS[core][panel][chip]
    return 0 if parent < 0 else 1 + depth(core, panel, parent)


def senders(core, panel, direction):
    parents = PARENTS[core][panel]
    return [n for n in range(16) if parents[neighbour(n, direction)] == n]


MESSAGES = (
    (0, 0, 0, 0),
    (0, 1, 0, 1),
    (0, 1, 1, 2),
    (1, 0, 0, 0),
    (1, 0, 1, 1),
    (1, 1, 0, 2),
    (1, 1, 1, 0),
    (2, 0, 0, 0),
    (2, 1, 0, 1),
    (2, 1, 1, 2),
)


def panels_kernel(
    a_ref, w_ref, r_ref, ct_ref, rows, slab, first_ct, fac, diag, stage, lead, inv, low,
    local_sem, row_send, row_recv, slab_send, slab_recv, fac_send, fac_recv, diag_sem,
):
    prow, pcol = lax.axis_index("prow"), lax.axis_index("pcol")
    z, core = prow // 2, prow % 2
    y, x = pcol // 4, pcol % 4
    is_root = jnp.logical_and(prow == 0, pcol == 0)
    gives_diag = jnp.logical_and(prow == 1, pcol == 1)

    def device(pz, pc, py, px):
        return {"prow": pz * 2 + pc, "pcol": py * 4 + px}

    def on_line(axis, step):
        if axis == "x":
            return device(z, core, y, (x + step) % 4)
        if axis == "y":
            return device(z, core, (y + step) % 4, x)
        return device((z + step) % 4, core, y, x)

    sibling = device(z, 1 - core, y, x)

    barrier = pltpu.get_barrier_semaphore()
    for axis in "xyz":
        for step in (1, 2, 3):
            pl.semaphore_signal(barrier, 1, device_id=on_line(axis, step), device_id_type=MESH)
    pl.semaphore_signal(barrier, 1, device_id=sibling, device_id_type=MESH)

    @pl.when(is_root)
    def _():
        pl.semaphore_signal(barrier, 1, device_id={"prow": 1, "pcol": 1}, device_id_type=MESH)

    pl.semaphore_wait(barrier, 10 + jnp.where(gives_diag, 1, 0))

    index = core * 16 + pcol
    gives = [[None] * 4 for _ in range(2)]
    for k in range(2):
        for d in range(4):
            flag = jnp.int32(0)
            for c in range(2):
                for n in senders(c, k, d):
                    flag = flag + jnp.where(index == c * 16 + n, 1, 0)
            gives[k][d] = flag == 1
    depths = []
    for k in range(2):
        value = jnp.int32(0)
        for c in range(2):
            for n in range(16):
                value = value + jnp.where(index == c * 16 + n, depth(c, k, n), 0)
        depths.append(value)
    slab_depths = (z + core, (4 - z) % 4 + 1 - core)
    fac_depth = core
    for coordinate in (x, y, z):
        fac_depth = fac_depth + jnp.where(coordinate != 0, 1, 0)
    targets = (on_line("x", 1), on_line("x", 3), on_line("y", 1), on_line("y", 3))

    def row_copy(src, k, d, first, count):
        piece = pl.ds(first, count)
        return pltpu.make_async_remote_copy(
            src_ref=src.at[piece, pl.ds(0, NB)] if src is a_ref else rows.at[k, piece, :],
            dst_ref=rows.at[k, piece, :],
            send_sem=row_send.at[k, d],
            recv_sem=row_recv.at[k, first // CHUNK if count == CHUNK else 0],
            device_id=targets[d],
            device_id_type=MESH,
        )

    def slab_copy(src, s, slot, first, count):
        piece = pl.ds(first, count)
        step = 1 if s == 0 else 3
        return pltpu.make_async_remote_copy(
            src_ref=a_ref.at[piece, :] if src is a_ref else slab.at[s, piece, :],
            dst_ref=slab.at[s, piece, :],
            send_sem=slab_send.at[s, slot],
            recv_sem=slab_recv.at[s, first // STRIP if count == STRIP else 0],
            device_id=on_line("z", step) if slot == 0 else sibling,
            device_id_type=MESH,
        )

    along = (
        jnp.logical_and(core == 0, z < 3),
        jnp.logical_and(core == 1, z != 1),
    )
    across = (core == 0, core == 1)

    def own_rows(k):
        return pltpu.make_async_copy(a_ref.at[:, pl.ds(0, NB)], rows.at[k], local_sem.at[k])

    def own_slab(s):
        return pltpu.make_async_copy(a_ref.at[pl.ds(0, NB), :], slab.at[s], local_sem.at[2 + s])

    def diag_copy():
        return pltpu.make_async_remote_copy(
            src_ref=a_ref.at[pl.ds(0, NB), pl.ds(0, NB)],
            dst_ref=diag,
            send_sem=diag_sem.at[0],
            recv_sem=diag_sem.at[1],
            device_id={"prow": 0, "pcol": 0},
            device_id_type=MESH,
        )

    def own_block():
        return pltpu.make_async_copy(a_ref, w_ref, local_sem.at[4])

    own_block().start()

    @pl.when(gives_diag)
    def _():
        diag_copy().start()

    for s in range(2):
        @pl.when(prow == s)
        def _(s=s):
            own_slab(s).start()

    for k in range(2):
        @pl.when(pcol == k)
        def _(k=k):
            own_rows(k).start()

            def send(i, carry):
                for d in range(4):
                    @pl.when(gives[k][d])
                    def _(d=d):
                        row_copy(a_ref, k, d, i * CHUNK, CHUNK).start()
                return carry

            lax.fori_loop(0, CHUNKS, send, 0)

    for s in range(2):
        @pl.when(prow == s)
        def _(s=s):
            def send(j, carry):
                slab_copy(a_ref, s, 0, j * STRIP, STRIP).start()
                slab_copy(a_ref, s, 1, j * STRIP, STRIP).start()
                return carry

            lax.fori_loop(0, STRIPS, send, 0)

    def pass_rows(tick):
        for k in range(2):
            i = tick - LAG * depths[k]
            here = jnp.logical_and(i >= 0, i < CHUNKS)

            @pl.when(jnp.logical_and(here, pcol != k))
            def _(k=k, i=i):
                row_copy(None, k, 0, i * CHUNK, CHUNK).wait_recv()
                for d in range(4):
                    @pl.when(gives[k][d])
                    def _(d=d):
                        row_copy(None, k, d, i * CHUNK, CHUNK).start()

    def pass_slab(tick):
        for s in range(2):
            j = tick - LAG * slab_depths[s]
            here = jnp.logical_and(j >= 0, j < STRIPS)
            here = jnp.logical_and(here, jnp.logical_not(is_root))

            @pl.when(jnp.logical_and(here, prow != s))
            def _(s=s, j=j):
                slab_copy(None, s, 0, j * STRIP, STRIP).wait_recv()

                @pl.when(along[s])
                def _():
                    slab_copy(None, s, 0, j * STRIP, STRIP).start()

                @pl.when(across[s])
                def _():
                    slab_copy(None, s, 1, j * STRIP, STRIP).start()

    where = {"x": x, "y": y, "z": z}

    def fac_targets(q):
        order = ("xyz", "yzx", "zxy")[MESSAGES[q][3]]
        at = [where[a] == 0 for a in order]
        first = jnp.logical_and(core == 0, jnp.logical_and(at[1], at[2]))
        conditions = (
            jnp.logical_and(first, at[0]),
            first,
            jnp.logical_and(core == 0, at[2]),
        )
        found = []
        for stage_index, axis in enumerate(order):
            for step in (2, 1, 3):
                found.append((conditions[stage_index], on_line(axis, step)))
        found.append((core == 0, sibling))
        return found

    def fac_copy(q, slot, target):
        m, i, j, _ = MESSAGES[q]
        piece = fac.at[m, pl.ds(i * 128, 128), pl.ds(j * 128, 128)]
        return pltpu.make_async_remote_copy(
            src_ref=piece,
            dst_ref=piece,
            send_sem=fac_send.at[q, slot],
            recv_sem=fac_recv.at[q],
            device_id=target,
            device_id_type=MESH,
        )

    def fac_start(q):
        for slot, (condition, target) in enumerate(fac_targets(q)):
            @pl.when(condition)
            def _(slot=slot, target=target):
                fac_copy(q, slot, target).start()

    def fac_pass(queue):
        @pl.when(jnp.logical_not(is_root))
        def _():
            for q in queue:
                fac_copy(q, 0, sibling).wait_recv()
                fac_start(q)

    for m in (0, 2):
        fac[m, 0:128, 128:256] = jnp.zeros((128, 128), F32)

    @pl.when(is_root)
    def _():
        own_slab(0).wait()
        stage[...] = slab[0, :, 0:NB]

        def panel(k, carry):
            lead[...] = stage[0:128, 0:128]

            def half(h, inner):
                inv[h] = chol128(lead[...])

                @pl.when(h == 0)
                def _():
                    low[...] = mmt(stage[128:256, 0:128], inv[0])
                    lead[...] = stage[128:256, 128:256] - mmt(low[...], low[...])

                return inner

            lax.fori_loop(0, 2, half, 0)
            fac[2 * k, 0:128, 0:128] = inv[0]
            fac[2 * k, 128:256, 128:256] = inv[1]
            fac[2 * k, 128:256, 0:128] = -mm(inv[1], mm(low[...], inv[0]))

            @pl.when(k == 0)
            def _():
                for q in (0, 1, 2):
                    fac_start(q)

                def arrive(j, inner):
                    slab_copy(None, 1, 0, j * STRIP, STRIP).wait_recv()
                    return inner

                lax.fori_loop(0, STRIPS, arrive, 0)
                below = mmt(slab[1, :, 0:NB], fac[0])
                fac[1] = below
                for q in (3, 4, 5, 6):
                    fac_start(q)
                diag_copy().wait_recv()
                stage[...] = diag[...] - mmt(below, below)

            @pl.when(k == 1)
            def _():
                for q in (7, 8, 9):
                    fac_start(q)

            return carry

        lax.fori_loop(0, 2, panel, 0)

    for k in range(2):
        @pl.when(pcol == k)
        def _(k=k):
            own_rows(k).wait()

    @pl.when(jnp.logical_and(prow == 0, jnp.logical_not(is_root)))
    def _():
        own_slab(0).wait()

    @pl.when(prow == 1)
    def _():
        own_slab(1).wait()

    own_block().wait()

    def step(tick, carry):
        pass_rows(tick)
        pass_slab(tick)

        @pl.when(tick == FIRST_FACTOR + LAG * fac_depth)
        def _():
            fac_pass((0, 1, 2, 3, 4, 5, 6))

        @pl.when(tick == SECOND_FACTOR + LAG * fac_depth)
        def _():
            fac_pass((7, 8, 9))

        @pl.when(jnp.logical_and(tick >= COLUMNS_TICK, tick < COLUMNS_TICK + COLS // NB))
        def _():
            tile = pl.ds(pl.multiple_of((tick - COLUMNS_TICK) * NB, NB), NB)
            first = mm(fac[0], slab[0, :, tile])
            high, low_part = split(first)
            first_ct[0, :, tile] = high
            first_ct[1, :, tile] = low_part
            ct_ref[:, tile] = slab[1, :, tile] - mm(fac[1], first)

        @pl.when(jnp.logical_and(tick >= BLOCKS_TICK, (tick - BLOCKS_TICK) % 2 == 0))
        def _():
            i = (tick - BLOCKS_TICK) // 2
            block = pl.ds(pl.multiple_of(i * NB, NB), NB)
            first = mmt(rows[0, block, :], fac[0])
            r_ref[block, :] = rows[1, block, :] - mmt(first, fac[1])
            w_ref[block, :] = w_ref[block, :] - three(first, first_ct[0], first_ct[1])

            @pl.when(pcol == 0)
            def _():
                down = lax.broadcasted_iota(jnp.int32, (NB, NB), 0)
                right = lax.broadcasted_iota(jnp.int32, (NB, NB), 1)
                keep = jnp.logical_or(i * 8 + prow > 0, right <= down)
                w_ref[block, 0:NB] = jnp.where(keep, first, 0.0)

        return carry

    lax.fori_loop(0, TICKS, step, 0)

    def columns(j, carry):
        tile = pl.ds(pl.multiple_of(j * NB, NB), NB)
        ct_ref[:, tile] = mm(fac[2], ct_ref[:, tile])
        return carry

    lax.fori_loop(0, COLS // NB, columns, 0)

    def second(j, carry):
        block = pl.ds(pl.multiple_of(j * NB, NB), NB)
        r_ref[block, :] = mmt(r_ref[block, :], fac[2])
        return carry

    lax.fori_loop(0, ROWS // NB, second, 0)

    for k in range(2):
        for d in range(4):
            @pl.when(gives[k][d])
            def _(k=k, d=d):
                row_copy(None, k, d, 0, ROWS).wait_send()

    for s in range(2):
        for slot, condition in enumerate((along[s], across[s])):
            @pl.when(condition)
            def _(s=s, slot=slot):
                slab_copy(None, s, slot, 0, NB).wait_send()

    for q in range(len(MESSAGES)):
        for slot, (condition, target) in enumerate(fac_targets(q)):
            @pl.when(condition)
            def _(q=q, slot=slot, target=target):
                fac_copy(q, slot, target).wait_send()

    @pl.when(gives_diag)
    def _():
        diag_copy().wait_send()


def make_panels(matrix):
    dma = pltpu.SemaphoreType.DMA
    vmem = pl.BlockSpec(memory_space=pltpu.VMEM)
    return pl.pallas_call(
        panels_kernel,
        out_shape=(
            jax.ShapeDtypeStruct((ROWS, COLS), F32),
            jax.ShapeDtypeStruct((ROWS, NB), F32),
            jax.ShapeDtypeStruct((NB, COLS), F32),
        ),
        in_specs=[pl.BlockSpec(memory_space=pl.ANY)],
        out_specs=(vmem, vmem, vmem),
        scratch_shapes=[
            pltpu.VMEM((2, ROWS, NB), F32),
            pltpu.VMEM((2, NB, COLS), F32),
            pltpu.VMEM((2, NB, COLS), BF16),
            pltpu.VMEM((3, NB, NB), F32),
            pltpu.VMEM((NB, NB), F32),
            pltpu.VMEM((NB, NB), F32),
            pltpu.VMEM((128, 128), F32),
            pltpu.VMEM((2, 128, 128), F32),
            pltpu.VMEM((128, 128), F32),
            dma((5,)),
            dma((2, 4)),
            dma((2, CHUNKS)),
            dma((2, 2)),
            dma((2, STRIPS)),
            dma((len(MESSAGES), 10)),
            dma((len(MESSAGES),)),
            dma((2,)),
        ],
        compiler_params=pltpu.CompilerParams(
            collective_id=0, has_side_effects=True, vmem_limit_bytes=36 * 2**20
        ),
        cost_estimate=pl.CostEstimate(
            flops=2 * 3 * ROWS * NB * COLS, bytes_accessed=2**24, transcendentals=0
        ),
        name="panels",
    )(matrix)


def update_kernel(place, w_ref, r_ref, ct_ref, out_ref, c_high, c_low):
    i = pl.program_id(0)

    @pl.when(i == 0)
    def _():
        def cut(j, carry):
            strip = pl.ds(pl.multiple_of(j * 64, 64), 64)
            c_high[strip, :], c_low[strip, :] = split(ct_ref[strip, :])
            return carry

        lax.fori_loop(0, NB // 64, cut, 0)

    prow, pcol = place[0], place[1]
    row_block = i * 8 + prow
    block = pl.ds(pl.multiple_of(i * NB, NB), NB)
    out_ref[...] = w_ref[block, :] - three(r_ref[block, :], c_high[...], c_low[...])

    @pl.when(row_block < 2)
    def _():
        out_ref[:, NB:COLS] = jnp.zeros((NB, COLS - NB), F32)

        @pl.when(pcol > row_block)
        def _():
            out_ref[:, 0:NB] = jnp.zeros((NB, NB), F32)

    @pl.when(pcol == 0)
    def _():
        out_ref[:, 0:NB] = w_ref[block, 0:NB]

    @pl.when(jnp.logical_and(pcol == 1, row_block >= 1))
    def _():
        down = lax.broadcasted_iota(jnp.int32, (NB, NB), 0)
        right = lax.broadcasted_iota(jnp.int32, (NB, NB), 1)
        keep = jnp.logical_or(row_block > 1, right <= down)
        out_ref[:, 0:NB] = jnp.where(keep, r_ref[block, :], 0.0)


def update(first_update, row_panel, col_panel):
    place = jnp.stack([lax.axis_index("prow"), lax.axis_index("pcol")]).astype(jnp.int32)
    vmem = pl.BlockSpec(memory_space=pltpu.VMEM)
    return pl.pallas_call(
        update_kernel,
        out_shape=jax.ShapeDtypeStruct((ROWS, COLS), F32),
        grid=(ROWS // NB,),
        in_specs=[pl.BlockSpec(memory_space=pltpu.SMEM), vmem, vmem, vmem],
        out_specs=pl.BlockSpec((NB, COLS), lambda i: (i, 0)),
        scratch_shapes=[pltpu.VMEM((NB, COLS), BF16), pltpu.VMEM((NB, COLS), BF16)],
        compiler_params=pltpu.CompilerParams(vmem_limit_bytes=36 * 2**20),
        cost_estimate=pl.CostEstimate(
            flops=2 * 3 * ROWS * COLS * NB, bytes_accessed=2**24, transcendentals=0
        ),
        name="update",
    )(place, first_update, row_panel, col_panel)


def body(matrix):
    first_update, row_panel, col_panel = make_panels(matrix)
    return update(first_update, row_panel, col_panel)


def solution(mesh):
    spec = P("prow", "pcol")
    return jax.shard_map(body, mesh=mesh, in_specs=(spec,), out_specs=spec, check_vma=False)
```

```python
import jax
import jax.numpy as jnp
from jax import lax
from jax.experimental import pallas as pl
from jax.experimental.pallas import tpu as pltpu

P = jax.sharding.PartitionSpec
MESH = pl.DeviceIdType.MESH
HI = lax.Precision.HIGHEST
F32 = jnp.float32
BF16 = jnp.bfloat16
NB = 256
HALF = NB // 2
ROWS = 2560
COLS = 1280
CHUNK = 64
CHUNKS = ROWS // CHUNK
STRIP = 16
STRIPS = NB // STRIP
BLOCKS = (3, 4, 3)
FIRST_MESSAGE = (0, 3, 7)
PLACES = (25, 29, 42)
ITEMS = CHUNKS + len(PLACES)
LAG = 4
DEEPEST = 5
TICKS = ITEMS + LAG * DEEPEST
SLAB_TICK = 12
AHEAD = 6
PUMP = 5


def mm(a, b):
    return lax.dot_general(a, b, (((1,), (0,)), ((), ())), precision=HI, preferred_element_type=F32)


def mmt(a, b):
    return lax.dot_general(a, b, (((1,), (1,)), ((), ())), precision=HI, preferred_element_type=F32)


def split(v):
    high = v.astype(BF16)
    return high, (v - high.astype(F32)).astype(BF16)


def three(a_high, a_low, b_high, b_low, contract=0):
    def dot(p, q):
        return lax.dot_general(p, q, (((1,), (contract,)), ((), ())), preferred_element_type=F32)

    return dot(a_high, b_high) + dot(a_high, b_low) + dot(a_low, b_high)


def three_t(a_high, a_low, b_high, b_low):
    return three(a_high, a_low, b_high, b_low, 1)


def full(v):
    return jnp.broadcast_to(v, (8, 128))

def leaf(w, start):
    lane = lax.broadcasted_iota(jnp.int32, (8, 128), 1)
    sub = lax.broadcasted_iota(jnp.int32, (8, 128), 0)
    other = (lane < 64) if start else (lane >= 64)
    rows = [w[8 * i:8 * i + 8, :] for i in range(8)]
    out = []
    for b in range(8):
        c = start + 8 * b
        bc = {i: [full(rows[i][:, c + k:c + k + 1]) for k in range(8)] for i in range(b, 8)}
        e = {(l, k): full(bc[b][k][l:l + 1, :]) for k in range(8) for l in range(k, 8)}
        u = [full(rows[b][k:k + 1, :]) for k in range(8)]
        done = jnp.zeros((8, 128), F32)
        for k in range(8):
            inv = 1.0 / e[k, k]
            for m in range(k + 1, 8):
                t = e[m, k] * inv
                for l in range(m, 8):
                    e[l, m] = e[l, m] - t * e[l, k]
                u[m] = u[m] - t * u[k]
                for i in range(b + 1, 8):
                    bc[i][m] = bc[i][m] - t * bc[i][k]
            scaled = u[k] * inv
            for i in range(b + 1, 8):
                rows[i] = rows[i] - bc[i][k] * scaled
            done = jnp.where(sub == k, u[k] * lax.rsqrt(e[k, k]), done)
        out.append(jnp.where(other, done, 0.0))
    return jnp.concatenate(out, axis=0)


def chol128(s, pump):
    r = lax.broadcasted_iota(jnp.int32, (64, 128), 0)
    c = lax.broadcasted_iota(jnp.int32, (64, 128), 1)
    low = jnp.where(c == r, 1.0, 0.0)
    high = jnp.where(c == r + 64, 1.0, 0.0)
    first = leaf(jnp.where(c < 64, s[:64], high), 0)
    pump(0)
    ma = pltpu.roll(first, 64, 1)
    l21 = mmt(jnp.where(c < 64, s[64:], 0.0), ma)
    s22 = mmt(l21, l21)
    z = jnp.zeros((64, 64), F32)
    s22 = jnp.concatenate([z, s22], axis=1)
    t = mm(l21, ma)
    second = leaf(jnp.where(c < 64, low, s[64:] - s22), 64)
    pump(1)
    low_part = mm(second[:, :64], high - t)
    return jnp.concatenate([ma, low_part], axis=0)


PARENTS = (
    (
        (-1, 0, 3, 0, 8, 9, 10, 11, 12, 8, 14, 8, 0, 12, 15, 12),
        (1, -1, 14, 15, 5, 1, 5, 6, 9, 13, 9, 15, 13, 1, 13, 14),
    ),
    (
        (-1, 5, 6, 7, 0, 4, 7, 4, 4, 5, 11, 7, 8, 9, 10, 11),
        (3, -1, 1, 2, 7, 6, 2, 3, 11, 10, 6, 10, 15, 14, 2, 3),
    ),
)


def neighbour(chip, direction):
    y, x = chip // 4, chip % 4
    if direction < 2:
        return y * 4 + (x + (1, 3)[direction]) % 4
    return (y + (1, 3)[direction - 2]) % 4 * 4 + x


def depth(core, panel, chip):
    parent = PARENTS[core][panel][chip]
    return 0 if parent < 0 else 1 + depth(core, panel, parent)


def handled_at(core, panel, chip):
    return depth(core, panel, chip) if chip in PARENTS[core][panel] else DEEPEST


def senders(core, panel, direction):
    parents = PARENTS[core][panel]
    return [n for n in range(16) if parents[neighbour(n, direction)] == n]


def panels_kernel(
    a_ref, w_ref, rows, slab, fac, leading, made, stage, lead, inv, low,
    local_sem, row_send, row_recv, slab_send, slab_recv,
    fac_send, fac_share, fac_give, fac_recv, lead_send, lead_recv,
):
    prow, pcol = lax.axis_index("prow"), lax.axis_index("pcol")
    z, core = prow // 2, prow % 2
    y, x = pcol // 4, pcol % 4
    both = jnp.logical_and
    is_root = both(core == 1, pcol == 0)
    gives_lead = (both(prow == 0, pcol == 0), both(prow == 1, pcol == 0), both(prow == 1, pcol == 1))

    def device(pz, pc, py, px):
        return {"prow": pz * 2 + pc, "pcol": py * 4 + px}

    def on_line(axis, step):
        if axis == "x":
            return device(z, core, y, (x + step) % 4)
        if axis == "y":
            return device(z, core, (y + step) % 4, x)
        return device((z + step) % 4, core, y, x)

    sibling = device(z, 1 - core, y, x)
    root = {"prow": z * 2 + 1, "pcol": 0}

    barrier = pltpu.get_barrier_semaphore()

    def greet(target):
        pl.semaphore_signal(barrier, 1, device_id=target, device_id_type=MESH)

    for axis in "xyz":
        for step in (1, 2, 3):
            greet(on_line(axis, step))
    greet(sibling)

    @pl.when(both(is_root, z > 0))
    def _():
        greet({"prow": 0, "pcol": 0})
        greet({"prow": 1, "pcol": 1})

    @pl.when(both(core == 0, pcol == 1))
    def _():
        greet(root)

    extra = jnp.where(is_root, 1, 0) + jnp.where(jnp.logical_or(gives_lead[0], gives_lead[2]), 3, 0)
    pl.semaphore_wait(barrier, 10 + extra)

    index = core * 16 + pcol
    gives = [[None] * 4 for _ in range(2)]
    for k in range(2):
        for d in range(4):
            flag = jnp.int32(0)
            for c in range(2):
                for n in senders(c, k, d):
                    flag = flag + jnp.where(index == c * 16 + n, 1, 0)
            gives[k][d] = flag == 1
    depths = []
    for k in range(2):
        value = jnp.int32(0)
        for c in range(2):
            for n in range(16):
                value = value + jnp.where(index == c * 16 + n, handled_at(c, k, n), 0)
        depths.append(value)
    targets = (on_line("x", 1), on_line("x", 3), on_line("y", 1), on_line("y", 3))

    def row_copy(src, k, d, first, count):
        piece = pl.ds(first, count)
        return pltpu.make_async_remote_copy(
            src_ref=src.at[piece, pl.ds(0, NB)] if src is a_ref else rows.at[k, piece, :],
            dst_ref=rows.at[k, piece, :],
            send_sem=row_send.at[k, d],
            recv_sem=row_recv.at[k, first // CHUNK if count == CHUNK else 0],
            device_id=targets[d],
            device_id_type=MESH,
        )

    on_ring = (core == 0, core == jnp.where(pcol == 0, 0, 1))
    along = (both(on_ring[0], z < 3), both(on_ring[1], z != 1))
    start_of_one = both(pcol == 0, z == 0)
    across = (on_ring[0], jnp.logical_or(both(start_of_one, core == 1), both(on_ring[1], jnp.logical_not(start_of_one))))
    slab_depths = (
        z + jnp.where(on_ring[0], 0, 1),
        (4 - z) % 4 + jnp.where(on_ring[1], 0, 1) + jnp.where(pcol == 0, 1, 0),
    )

    def slab_copy(src, s, slot, first, count):
        piece = pl.ds(first, count)
        step = 1 if s == 0 else 3
        return pltpu.make_async_remote_copy(
            src_ref=a_ref.at[piece, :] if src is a_ref else slab.at[s, piece, :],
            dst_ref=slab.at[s, piece, :],
            send_sem=slab_send.at[s, slot],
            recv_sem=slab_recv.at[s, first // STRIP if count == STRIP else 0],
            device_id=on_line("z", step) if slot == 0 else sibling,
            device_id_type=MESH,
        )

    def own_rows(k):
        return pltpu.make_async_copy(a_ref.at[:, pl.ds(0, NB)], rows.at[k], local_sem.at[k])

    def own_slab(s):
        return pltpu.make_async_copy(a_ref.at[pl.ds(0, NB), :], slab.at[s], local_sem.at[2 + s])

    def own_lead():
        return pltpu.make_async_copy(a_ref.at[pl.ds(0, NB), pl.ds(0, NB)], leading.at[1], local_sem.at[4])

    def own_block(i):
        piece = pl.ds(pl.multiple_of(i * NB, NB), NB)
        return pltpu.make_async_copy(a_ref.at[piece, :], w_ref.at[piece, :], local_sem.at[5 + i])

    def lead_copy(n, e, to_z):
        down, right, size = (0, 0, NB) if n == 1 else ((e + 1) // 2 * HALF, e // 2 * HALF, HALF)
        return pltpu.make_async_remote_copy(
            src_ref=a_ref.at[pl.ds(down, size), pl.ds(right, size)],
            dst_ref=leading.at[n, pl.ds(down, size), pl.ds(right, size)],
            send_sem=lead_send.at[n, e, to_z],
            recv_sem=lead_recv.at[n, e],
            device_id={"prow": 2 * to_z + 1, "pcol": 0},
            device_id_type=MESH,
        )

    def leads():
        for n in range(3):
            for e in range(1 if n == 1 else 3):
                for to_z in ((1, 3, 2) if n == 1 else (0, 1, 3, 2)):
                    yield n, e, to_z

    for n, e, to_z in leads():
        @pl.when(gives_lead[n])
        def _(n=n, e=e, to_z=to_z):
            lead_copy(n, e, to_z).start()

    @pl.when(gives_lead[1])
    def _():
        own_lead().start()

    for s in range(2):
        @pl.when(prow == s)
        def _(s=s):
            own_slab(s).start()

    for k in range(2):
        @pl.when(pcol == k)
        def _(k=k):
            own_rows(k).start()

    def send_chunk(src, k, i):
        for d in range(4):
            @pl.when(gives[k][d])
            def _(d=d):
                row_copy(src, k, d, i * CHUNK, CHUNK).start()

    def send_strip(src, s, j):
        @pl.when(along[s])
        def _():
            slab_copy(src, s, 0, j * STRIP, STRIP).start()

        @pl.when(across[s])
        def _():
            slab_copy(src, s, 1, j * STRIP, STRIP).start()

    def fac_block(ref, part, e):
        i, j = (e // 2, e % 2) if part == 1 else ((e + 1) // 2, e // 2)
        if not isinstance(e, int):
            i, j = pl.multiple_of(i * HALF, HALF), pl.multiple_of(j * HALF, HALF)
        else:
            i, j = i * HALF, j * HALF
        return ref.at[part, pl.ds(i, HALF), pl.ds(j, HALF)]

    def fac_copy(src, part, e, send_sem, target):
        return pltpu.make_async_remote_copy(
            src_ref=fac_block(src, part, e),
            dst_ref=fac_block(fac, part, e),
            send_sem=send_sem,
            recv_sem=fac_recv.at[FIRST_MESSAGE[part] + e],
            device_id=target,
            device_id_type=MESH,
        )

    def each_fac(part, k, act):
        e = core * 2 + k
        for d in range(4):
            @pl.when(gives[k][d])
            def _(d=d):
                act(fac_copy(fac, part, e, fac_send.at[part, k, d], targets[d]))
        act(fac_copy(fac, part, e, fac_share.at[part, k], sibling))

    def root_fac(part, act):
        for e, target in ((0, sibling), (1, {"prow": z * 2, "pcol": 1}), (3, {"prow": z * 2 + 1, "pcol": 1})):
            if e < BLOCKS[part]:
                act(fac_copy(made, part, e, fac_give.at[part, e], target))

    def begin(copy):
        copy.start()

    def finish(copy):
        copy.wait_send()

    def give_part(part):
        root_fac(part, begin)
        i, j = (1, 0) if part == 1 else (1, 1)
        span = (part, pl.ds(i * HALF, HALF), pl.ds(j * HALF, HALF))
        fac[span] = made[span]
        each_fac(part, 0, begin)

    def pass_rows(tick):
        for k in range(2):
            n = tick - LAG * depths[k]
            skips = jnp.int32(0)
            special = n < 0
            for place in PLACES:
                skips = skips + jnp.where(n > place, 1, 0)
                special = jnp.logical_or(special, n == place)
            i = n - skips
            here = both(jnp.logical_not(special), n < ITEMS)
            mine = both(here, pcol == k)
            if k == 0:
                mine = both(mine, jnp.logical_not(is_root))

            @pl.when(both(here, pcol != k))
            def _(k=k, i=i):
                row_copy(None, k, 0, i * CHUNK, CHUNK).wait_recv()
                send_chunk(None, k, i)

            @pl.when(mine)
            def _(k=k, i=i):
                send_chunk(a_ref, k, i)

            for part, place in enumerate(PLACES):
                now = both(n == place, core * 2 + k < BLOCKS[part])
                if k == 0:
                    now = both(now, jnp.logical_not(is_root))

                @pl.when(now)
                def _(k=k, part=part):
                    fac_copy(fac, part, core * 2 + k, fac_share.at[part, k], sibling).wait_recv()
                    each_fac(part, k, begin)

    def pass_slab(tick):
        for s in range(2):
            j = tick - SLAB_TICK - LAG * slab_depths[s]
            here = both(j >= 0, j < STRIPS)

            @pl.when(both(here, prow != s))
            def _(s=s, j=j):
                slab_copy(None, s, 0, j * STRIP, STRIP).wait_recv()
                send_strip(None, s, j)

            @pl.when(both(both(tick < STRIPS, prow == s), jnp.logical_not(is_root)))
            def _(s=s):
                send_strip(a_ref, s, tick)

    for part in (0, 2):
        fac[part, 0:HALF, HALF:NB] = jnp.zeros((HALF, HALF), F32)

    @pl.when(is_root)
    def _():
        def pump(first, count):
            def one(i, carry):
                @pl.when(i < CHUNKS)
                def _():
                    send_chunk(a_ref, 0, i)

                return carry

            lax.fori_loop(first, first + count, one, 0)

        pump(0, AHEAD)

        @pl.when(prow == 1)
        def _():
            def one(j, carry):
                send_strip(a_ref, 1, j)
                return carry

            lax.fori_loop(0, STRIPS, one, 0)

        lead_copy(0, 0, z).wait_recv()
        lead[...] = leading[0, 0:HALF, 0:HALF]

        def panel(k, carry):
            def half(h, inner):
                inv[h] = chol128(lead[...], lambda n: pump(AHEAD + (4 * k + 2 * h + n) * PUMP, PUMP))

                @pl.when(h == 0)
                def _():
                    @pl.when(k == 0)
                    def _():
                        for e in (1, 2):
                            lead_copy(0, e, z).wait_recv()
                        stage[HALF:NB, :] = leading[0, HALF:NB, :]

                    low[...] = mmt(stage[HALF:NB, 0:HALF], inv[0])
                    lead[...] = stage[HALF:NB, HALF:NB] - mmt(low[...], low[...])

                return inner

            lax.fori_loop(0, 2, half, 0)
            made[2 * k, 0:HALF, 0:HALF] = inv[0]
            made[2 * k, 0:HALF, HALF:NB] = jnp.zeros((HALF, HALF), F32)
            made[2 * k, HALF:NB, HALF:NB] = inv[1]
            made[2 * k, HALF:NB, 0:HALF] = -mm(inv[1], mm(low[...], inv[0]))

            @pl.when(k == 0)
            def _():
                give_part(0)

                @pl.when(prow == 1)
                def _():
                    own_lead().wait()

                @pl.when(prow != 1)
                def _():
                    lead_copy(1, 0, z).wait_recv()

                made[1] = mmt(leading[1], made[0])
                give_part(1)
                for e in range(3):
                    lead_copy(2, e, z).wait_recv()
                square = mmt(made[1], made[1])
                lead[...] = leading[2, 0:HALF, 0:HALF] - square[0:HALF, 0:HALF]
                stage[HALF:NB, :] = leading[2, HALF:NB, :] - square[HALF:NB, :]

            @pl.when(k == 1)
            def _():
                give_part(2)

            return carry

        lax.fori_loop(0, 2, panel, 0)

    for k in range(2):
        @pl.when(pcol == k)
        def _(k=k):
            own_rows(k).wait()

    for s in range(2):
        @pl.when(prow == s)
        def _(s=s):
            own_slab(s).wait()

    def step(tick, carry):
        pass_rows(tick)
        pass_slab(tick)

        @pl.when(both(tick % 2 == 1, tick < 2 * (ROWS // NB)))
        def _():
            own_block(tick // 2).start()

        return carry

    lax.fori_loop(0, TICKS, step, 0)

    for part in range(3):
        for k in range(2):
            other = (1 - core) * 2 + k

            @pl.when(other < BLOCKS[part])
            def _(part=part, k=k, other=other):
                fac_copy(fac, part, other, fac_share.at[part, k], sibling).wait_recv()

    def block_here(i, carry):
        own_block(i).wait()
        return carry

    lax.fori_loop(0, ROWS // NB, block_here, 0)

    for k in range(2):
        for d in range(4):
            @pl.when(gives[k][d])
            def _(k=k, d=d):
                row_copy(None, k, d, 0, ROWS).wait_send()

    for s in range(2):
        for slot, condition in enumerate((along[s], across[s])):
            @pl.when(condition)
            def _(s=s, slot=slot):
                slab_copy(None, s, slot, 0, NB).wait_send()

    for part in range(3):
        for k in range(2):
            @pl.when(core * 2 + k < BLOCKS[part])
            def _(part=part, k=k):
                each_fac(part, k, finish)

        @pl.when(is_root)
        def _(part=part):
            root_fac(part, finish)

    for n, e, to_z in leads():
        @pl.when(gives_lead[n])
        def _(n=n, e=e, to_z=to_z):
            lead_copy(n, e, to_z).wait_send()


def make_panels(matrix):
    dma = pltpu.SemaphoreType.DMA
    vmem = pl.BlockSpec(memory_space=pltpu.VMEM)
    return pl.pallas_call(
        panels_kernel,
        out_shape=(
            jax.ShapeDtypeStruct((ROWS, COLS), F32),
            jax.ShapeDtypeStruct((2, ROWS, NB), F32),
            jax.ShapeDtypeStruct((2, NB, COLS), F32),
            jax.ShapeDtypeStruct((3, NB, NB), F32),
        ),
        in_specs=[pl.BlockSpec(memory_space=pl.ANY)],
        out_specs=(vmem, vmem, vmem, vmem),
        scratch_shapes=[
            pltpu.VMEM((3, NB, NB), F32),
            pltpu.VMEM((3, NB, NB), F32),
            pltpu.VMEM((NB, NB), F32),
            pltpu.VMEM((HALF, HALF), F32),
            pltpu.VMEM((2, HALF, HALF), F32),
            pltpu.VMEM((HALF, HALF), F32),
            dma((5 + ROWS // NB,)),
            dma((2, 4)),
            dma((2, CHUNKS)),
            dma((2, 2)),
            dma((2, STRIPS)),
            dma((3, 2, 4)),
            dma((3, 2)),
            dma((3, 4)),
            dma((sum(BLOCKS),)),
            dma((3, 3, 4)),
            dma((3, 3)),
        ],
        compiler_params=pltpu.CompilerParams(
            collective_id=0, has_side_effects=True, vmem_limit_bytes=32 * 2**20
        ),
        cost_estimate=pl.CostEstimate(flops=2**30, bytes_accessed=2**24, transcendentals=0),
        name="panels",
    )(matrix)


def update_kernel(place, w_ref, rows, slab, fac, out_ref, c_high, c_low, f_split):
    i = pl.program_id(0)

    @pl.when(i == 0)
    def _():
        for part in range(3):
            f_split[part, 0], f_split[part, 1] = split(fac[part])

        def columns(j, carry):
            tile = pl.ds(pl.multiple_of(j * NB, NB), NB)
            first = three(f_split[0, 0], f_split[0, 1], *split(slab[0, :, tile]))
            high, low = split(first)
            c_high[0:NB, tile] = high
            c_low[0:NB, tile] = low
            rest = slab[1, :, tile] - three(f_split[1, 0], f_split[1, 1], high, low)
            high, low = split(three(f_split[2, 0], f_split[2, 1], *split(rest)))
            c_high[NB:2 * NB, tile] = high
            c_low[NB:2 * NB, tile] = low
            return carry

        lax.fori_loop(0, COLS // NB, columns, 0)

    prow, pcol = place[0], place[1]
    row_block = i * 8 + prow
    block = pl.ds(pl.multiple_of(i * NB, NB), NB)
    first = three_t(*split(rows[0, block, :]), f_split[0, 0], f_split[0, 1])
    first_high, first_low = split(first)
    rest = rows[1, block, :] - three_t(first_high, first_low, f_split[1, 0], f_split[1, 1])
    second = three_t(*split(rest), f_split[2, 0], f_split[2, 1])
    second_high, second_low = split(second)
    high = jnp.concatenate([first_high, second_high], axis=1)
    low = jnp.concatenate([first_low, second_low], axis=1)
    out_ref[...] = w_ref[block, :] - three(high, low, c_high[...], c_low[...])

    @pl.when(row_block < 2)
    def _():
        out_ref[...] = jnp.zeros((NB, COLS), F32)

    down = lax.broadcasted_iota(jnp.int32, (NB, NB), 0)
    right = lax.broadcasted_iota(jnp.int32, (NB, NB), 1)
    for k, panel in enumerate((first, second)):
        @pl.when(both_true(pcol == k, row_block >= k))
        def _(k=k, panel=panel):
            keep = jnp.logical_or(row_block > k, right <= down)
            out_ref[:, 0:NB] = jnp.where(keep, panel, 0.0)


def both_true(a, b):
    return jnp.logical_and(a, b)


def update(matrix, rows, slab, fac):
    place = jnp.stack([lax.axis_index("prow"), lax.axis_index("pcol")]).astype(jnp.int32)
    vmem = pl.BlockSpec(memory_space=pltpu.VMEM)
    return pl.pallas_call(
        update_kernel,
        out_shape=jax.ShapeDtypeStruct((ROWS, COLS), F32),
        grid=(ROWS // NB,),
        in_specs=[pl.BlockSpec(memory_space=pltpu.SMEM), vmem, vmem, vmem, vmem],
        out_specs=pl.BlockSpec((NB, COLS), lambda i: (i, 0)),
        scratch_shapes=[
            pltpu.VMEM((2 * NB, COLS), BF16),
            pltpu.VMEM((2 * NB, COLS), BF16),
            pltpu.VMEM((3, 2, NB, NB), BF16),
        ],
        compiler_params=pltpu.CompilerParams(vmem_limit_bytes=32 * 2**20),
        cost_estimate=pl.CostEstimate(
            flops=2 * 3 * ROWS * COLS * 2 * NB, bytes_accessed=2**24, transcendentals=0
        ),
        name="update",
    )(place, matrix, rows, slab, fac)


def body(matrix):
    return update(*make_panels(matrix))


def solution(mesh):
    spec = P("prow", "pcol")
    return jax.shard_map(body, mesh=mesh, in_specs=(spec,), out_specs=spec, check_vma=False)
```

```python
import jax
import jax.numpy as jnp
from jax import lax
from jax.experimental import pallas as pl
from jax.experimental.pallas import tpu as pltpu

P = jax.sharding.PartitionSpec
MESH = pl.DeviceIdType.MESH
HI = lax.Precision.HIGHEST
F32 = jnp.float32
BF16 = jnp.bfloat16
NB = 256
HALF = NB // 2
ROWS = 2560
COLS = 1280
CHUNK = 64
CHUNKS = ROWS // CHUNK
STRIP = 16
STRIPS = NB // STRIP
BLOCKS = (3, 4, 3)
FIRST_MESSAGE = (0, 3, 7)
PLACES = (27, 30, 42)
ITEMS = CHUNKS + len(PLACES)
LAG = 4
DEEPEST = 5
TICKS = ITEMS + LAG * DEEPEST
SLAB_TICK = 12
FIRST_WORK = PLACES[0] + LAG * DEEPEST + 1
ROWS_WORK = TICKS - ROWS // NB
COLUMN_BLOCKS = COLS // NB
ROW_BLOCKS = ROWS // NB
AHEAD = 6
PUMP = 5


def mm(a, b):
    return lax.dot_general(a, b, (((1,), (0,)), ((), ())), precision=HI, preferred_element_type=F32)


def mmt(a, b):
    return lax.dot_general(a, b, (((1,), (1,)), ((), ())), precision=HI, preferred_element_type=F32)


def split(v):
    high = v.astype(BF16)
    return high, (v - high.astype(F32)).astype(BF16)


def three(a_high, a_low, b_high, b_low, contract=0):
    def dot(p, q):
        return lax.dot_general(p, q, (((1,), (contract,)), ((), ())), preferred_element_type=F32)

    return dot(a_high, b_high) + dot(a_high, b_low) + dot(a_low, b_high)


def three_t(a_high, a_low, b_high, b_low):
    return three(a_high, a_low, b_high, b_low, 1)


def full(v):
    return jnp.broadcast_to(v, (8, 128))

def leaf(w, start):
    lane = lax.broadcasted_iota(jnp.int32, (8, 128), 1)
    sub = lax.broadcasted_iota(jnp.int32, (8, 128), 0)
    other = (lane < 64) if start else (lane >= 64)
    rows = [w[8 * i:8 * i + 8, :] for i in range(8)]
    out = []
    for b in range(8):
        c = start + 8 * b
        bc = {i: [full(rows[i][:, c + k:c + k + 1]) for k in range(8)] for i in range(b, 8)}
        e = {(l, k): full(bc[b][k][l:l + 1, :]) for k in range(8) for l in range(k, 8)}
        u = [full(rows[b][k:k + 1, :]) for k in range(8)]
        done = jnp.zeros((8, 128), F32)
        for k in range(8):
            inv = 1.0 / e[k, k]
            for m in range(k + 1, 8):
                t = e[m, k] * inv
                for l in range(m, 8):
                    e[l, m] = e[l, m] - t * e[l, k]
                u[m] = u[m] - t * u[k]
                for i in range(b + 1, 8):
                    bc[i][m] = bc[i][m] - t * bc[i][k]
            scaled = u[k] * inv
            for i in range(b + 1, 8):
                rows[i] = rows[i] - bc[i][k] * scaled
            done = jnp.where(sub == k, u[k] * lax.rsqrt(e[k, k]), done)
        out.append(jnp.where(other, done, 0.0))
    return jnp.concatenate(out, axis=0)


def chol128(s, pump):
    r = lax.broadcasted_iota(jnp.int32, (64, 128), 0)
    c = lax.broadcasted_iota(jnp.int32, (64, 128), 1)
    low = jnp.where(c == r, 1.0, 0.0)
    high = jnp.where(c == r + 64, 1.0, 0.0)
    first = leaf(jnp.where(c < 64, s[:64], high), 0)
    pump(0)
    ma = pltpu.roll(first, 64, 1)
    l21 = mmt(jnp.where(c < 64, s[64:], 0.0), ma)
    s22 = mmt(l21, l21)
    z = jnp.zeros((64, 64), F32)
    s22 = jnp.concatenate([z, s22], axis=1)
    t = mm(l21, ma)
    second = leaf(jnp.where(c < 64, low, s[64:] - s22), 64)
    pump(1)
    low_part = mm(second[:, :64], high - t)
    return jnp.concatenate([ma, low_part], axis=0)


PARENTS = (
    (
        (-1, 0, 3, 0, 8, 9, 10, 11, 12, 8, 14, 8, 0, 12, 15, 12),
        (1, -1, 14, 15, 5, 1, 5, 6, 9, 13, 9, 15, 13, 1, 13, 14),
    ),
    (
        (-1, 5, 6, 7, 0, 4, 7, 4, 4, 5, 11, 7, 8, 9, 10, 11),
        (3, -1, 1, 2, 7, 6, 2, 3, 11, 10, 6, 10, 15, 14, 2, 3),
    ),
)


def neighbour(chip, direction):
    y, x = chip // 4, chip % 4
    if direction < 2:
        return y * 4 + (x + (1, 3)[direction]) % 4
    return (y + (1, 3)[direction - 2]) % 4 * 4 + x


def depth(core, panel, chip):
    parent = PARENTS[core][panel][chip]
    return 0 if parent < 0 else 1 + depth(core, panel, parent)


def handled_at(core, panel, chip):
    return depth(core, panel, chip) if chip in PARENTS[core][panel] else DEEPEST


def senders(core, panel, direction):
    parents = PARENTS[core][panel]
    return [n for n in range(16) if parents[neighbour(n, direction)] == n]


def panels_kernel(
    a_ref, w_ref, r_high, r_low, c_high, c_low, rows, slab, fac, fac_split, rest, leading, made, stage, lead, inv, low,
    local_sem, row_send, row_recv, slab_send, slab_recv,
    fac_send, fac_share, fac_give, fac_recv, lead_send, lead_recv,
):
    prow, pcol = lax.axis_index("prow"), lax.axis_index("pcol")
    z, core = prow // 2, prow % 2
    y, x = pcol // 4, pcol % 4
    both = jnp.logical_and
    is_root = both(core == 1, pcol == 0)
    gives_lead = (both(prow == 0, pcol == 0), both(prow == 1, pcol == 0), both(prow == 1, pcol == 1))

    def device(pz, pc, py, px):
        return {"prow": pz * 2 + pc, "pcol": py * 4 + px}

    def on_line(axis, step):
        if axis == "x":
            return device(z, core, y, (x + step) % 4)
        if axis == "y":
            return device(z, core, (y + step) % 4, x)
        return device((z + step) % 4, core, y, x)

    sibling = device(z, 1 - core, y, x)
    root = {"prow": z * 2 + 1, "pcol": 0}

    barrier = pltpu.get_barrier_semaphore()

    def greet(target):
        pl.semaphore_signal(barrier, 1, device_id=target, device_id_type=MESH)

    for axis in "xyz":
        for step in (1, 2, 3):
            greet(on_line(axis, step))
    greet(sibling)

    @pl.when(both(is_root, z > 0))
    def _():
        greet({"prow": 0, "pcol": 0})
        greet({"prow": 1, "pcol": 1})

    @pl.when(both(core == 0, pcol == 1))
    def _():
        greet(root)

    extra = jnp.where(is_root, 1, 0) + jnp.where(jnp.logical_or(gives_lead[0], gives_lead[2]), 3, 0)
    pl.semaphore_wait(barrier, 10 + extra)

    index = core * 16 + pcol
    gives = [[None] * 4 for _ in range(2)]
    for k in range(2):
        for d in range(4):
            flag = jnp.int32(0)
            for c in range(2):
                for n in senders(c, k, d):
                    flag = flag + jnp.where(index == c * 16 + n, 1, 0)
            gives[k][d] = flag == 1
    depths = []
    for k in range(2):
        value = jnp.int32(0)
        for c in range(2):
            for n in range(16):
                value = value + jnp.where(index == c * 16 + n, handled_at(c, k, n), 0)
        depths.append(value)
    targets = (on_line("x", 1), on_line("x", 3), on_line("y", 1), on_line("y", 3))

    def row_copy(src, k, d, first, count):
        piece = pl.ds(first, count)
        return pltpu.make_async_remote_copy(
            src_ref=src.at[piece, pl.ds(0, NB)] if src is a_ref else rows.at[k, piece, :],
            dst_ref=rows.at[k, piece, :],
            send_sem=row_send.at[k, d],
            recv_sem=row_recv.at[k, first // CHUNK if count == CHUNK else 0],
            device_id=targets[d],
            device_id_type=MESH,
        )

    on_ring = (core == 0, core == jnp.where(pcol == 0, 0, 1))
    along = (both(on_ring[0], z < 3), both(on_ring[1], z != 1))
    start_of_one = both(pcol == 0, z == 0)
    across = (on_ring[0], jnp.logical_or(both(start_of_one, core == 1), both(on_ring[1], jnp.logical_not(start_of_one))))
    slab_depths = (
        z + jnp.where(on_ring[0], 0, 1),
        (4 - z) % 4 + jnp.where(on_ring[1], 0, 1) + jnp.where(pcol == 0, 1, 0),
    )

    def slab_copy(src, s, slot, first, count):
        piece = pl.ds(first, count)
        step = 1 if s == 0 else 3
        return pltpu.make_async_remote_copy(
            src_ref=a_ref.at[piece, :] if src is a_ref else slab.at[s, piece, :],
            dst_ref=slab.at[s, piece, :],
            send_sem=slab_send.at[s, slot],
            recv_sem=slab_recv.at[s, first // STRIP if count == STRIP else 0],
            device_id=on_line("z", step) if slot == 0 else sibling,
            device_id_type=MESH,
        )

    def own_rows(k):
        return pltpu.make_async_copy(a_ref.at[:, pl.ds(0, NB)], rows.at[k], local_sem.at[k])

    def own_slab(s):
        return pltpu.make_async_copy(a_ref.at[pl.ds(0, NB), :], slab.at[s], local_sem.at[2 + s])

    def own_lead():
        return pltpu.make_async_copy(a_ref.at[pl.ds(0, NB), pl.ds(0, NB)], leading.at[1], local_sem.at[4])

    def own_block(i):
        piece = pl.ds(pl.multiple_of(i * CHUNK, CHUNK), CHUNK)
        return pltpu.make_async_copy(a_ref.at[piece, :], w_ref.at[piece, :], local_sem.at[5 + i])

    def lead_copy(n, e, to_z):
        down, right, size = (0, 0, NB) if n == 1 else ((e + 1) // 2 * HALF, e // 2 * HALF, HALF)
        return pltpu.make_async_remote_copy(
            src_ref=a_ref.at[pl.ds(down, size), pl.ds(right, size)],
            dst_ref=leading.at[n, pl.ds(down, size), pl.ds(right, size)],
            send_sem=lead_send.at[n, e, to_z],
            recv_sem=lead_recv.at[n, e],
            device_id={"prow": 2 * to_z + 1, "pcol": 0},
            device_id_type=MESH,
        )

    def leads():
        for n in range(3):
            for e in range(1 if n == 1 else 3):
                for to_z in ((1, 3, 2) if n == 1 else (0, 1, 3, 2)):
                    yield n, e, to_z

    for n, e, to_z in leads():
        @pl.when(gives_lead[n])
        def _(n=n, e=e, to_z=to_z):
            lead_copy(n, e, to_z).start()

    @pl.when(gives_lead[1])
    def _():
        own_lead().start()

    for s in range(2):
        @pl.when(prow == s)
        def _(s=s):
            own_slab(s).start()

    for k in range(2):
        @pl.when(pcol == k)
        def _(k=k):
            own_rows(k).start()

    def send_chunk(src, k, i):
        for d in range(4):
            @pl.when(gives[k][d])
            def _(d=d):
                row_copy(src, k, d, i * CHUNK, CHUNK).start()

    def send_strip(src, s, j):
        @pl.when(along[s])
        def _():
            slab_copy(src, s, 0, j * STRIP, STRIP).start()

        @pl.when(across[s])
        def _():
            slab_copy(src, s, 1, j * STRIP, STRIP).start()

    def fac_block(ref, part, e):
        i, j = (e // 2, e % 2) if part == 1 else ((e + 1) // 2, e // 2)
        if not isinstance(e, int):
            i, j = pl.multiple_of(i * HALF, HALF), pl.multiple_of(j * HALF, HALF)
        else:
            i, j = i * HALF, j * HALF
        return ref.at[part, pl.ds(i, HALF), pl.ds(j, HALF)]

    def fac_copy(src, part, e, send_sem, target):
        return pltpu.make_async_remote_copy(
            src_ref=fac_block(src, part, e),
            dst_ref=fac_block(fac, part, e),
            send_sem=send_sem,
            recv_sem=fac_recv.at[FIRST_MESSAGE[part] + e],
            device_id=target,
            device_id_type=MESH,
        )

    def each_fac(part, k, act):
        e = core * 2 + k
        for d in range(4):
            @pl.when(gives[k][d])
            def _(d=d):
                act(fac_copy(fac, part, e, fac_send.at[part, k, d], targets[d]))
        act(fac_copy(fac, part, e, fac_share.at[part, k], sibling))

    def root_fac(part, act):
        for e, target in ((0, sibling), (1, {"prow": z * 2, "pcol": 1}), (3, {"prow": z * 2 + 1, "pcol": 1})):
            if e < BLOCKS[part]:
                act(fac_copy(made, part, e, fac_give.at[part, e], target))

    def begin(copy):
        copy.start()

    def finish(copy):
        copy.wait_send()

    def give_part(part):
        root_fac(part, begin)
        i, j = (1, 0) if part == 1 else (1, 1)
        span = (part, pl.ds(i * HALF, HALF), pl.ds(j * HALF, HALF))
        fac[span] = made[span]
        each_fac(part, 0, begin)

    def pass_rows(tick):
        for k in range(2):
            n = tick - LAG * depths[k]
            skips = jnp.int32(0)
            special = n < 0
            for place in PLACES:
                skips = skips + jnp.where(n > place, 1, 0)
                special = jnp.logical_or(special, n == place)
            i = n - skips
            here = both(jnp.logical_not(special), n < ITEMS)
            mine = both(here, pcol == k)
            if k == 0:
                mine = both(mine, jnp.logical_not(is_root))

            @pl.when(both(here, pcol != k))
            def _(k=k, i=i):
                row_copy(None, k, 0, i * CHUNK, CHUNK).wait_recv()
                send_chunk(None, k, i)

            @pl.when(mine)
            def _(k=k, i=i):
                send_chunk(a_ref, k, i)

            for part, place in enumerate(PLACES):
                now = both(n == place, core * 2 + k < BLOCKS[part])
                if k == 0:
                    now = both(now, jnp.logical_not(is_root))

                @pl.when(now)
                def _(k=k, part=part):
                    fac_copy(fac, part, core * 2 + k, fac_share.at[part, k], sibling).wait_recv()
                    each_fac(part, k, begin)

    def pass_slab(tick):
        for s in range(2):
            j = tick - SLAB_TICK - LAG * slab_depths[s]
            here = both(j >= 0, j < STRIPS)

            @pl.when(both(here, prow != s))
            def _(s=s, j=j):
                slab_copy(None, s, 0, j * STRIP, STRIP).wait_recv()
                send_strip(None, s, j)

            @pl.when(both(both(tick < STRIPS, prow == s), jnp.logical_not(is_root)))
            def _(s=s):
                send_strip(a_ref, s, tick)

    for part in (0, 2):
        fac[part, 0:HALF, HALF:NB] = jnp.zeros((HALF, HALF), F32)

    @pl.when(is_root)
    def _():
        def pump(first, count):
            def one(i, carry):
                @pl.when(i < CHUNKS)
                def _():
                    send_chunk(a_ref, 0, i)

                return carry

            lax.fori_loop(first, first + count, one, 0)

        pump(0, AHEAD)

        @pl.when(prow == 1)
        def _():
            def one(j, carry):
                send_strip(a_ref, 1, j)
                return carry

            lax.fori_loop(0, STRIPS, one, 0)

        lead_copy(0, 0, z).wait_recv()
        lead[...] = leading[0, 0:HALF, 0:HALF]

        def panel(k, carry):
            def half(h, inner):
                inv[h] = chol128(lead[...], lambda n: pump(AHEAD + (4 * k + 2 * h + n) * PUMP, PUMP))

                @pl.when(h == 0)
                def _():
                    @pl.when(k == 0)
                    def _():
                        for e in (1, 2):
                            lead_copy(0, e, z).wait_recv()
                        stage[HALF:NB, :] = leading[0, HALF:NB, :]

                    low[...] = mmt(stage[HALF:NB, 0:HALF], inv[0])
                    lead[...] = stage[HALF:NB, HALF:NB] - mmt(low[...], low[...])

                return inner

            lax.fori_loop(0, 2, half, 0)
            made[2 * k, 0:HALF, 0:HALF] = inv[0]
            made[2 * k, 0:HALF, HALF:NB] = jnp.zeros((HALF, HALF), F32)
            made[2 * k, HALF:NB, HALF:NB] = inv[1]
            made[2 * k, HALF:NB, 0:HALF] = -mm(inv[1], mm(low[...], inv[0]))

            @pl.when(k == 0)
            def _():
                give_part(0)

                @pl.when(prow == 1)
                def _():
                    own_lead().wait()

                @pl.when(prow != 1)
                def _():
                    lead_copy(1, 0, z).wait_recv()

                made[1] = mmt(leading[1], made[0])
                give_part(1)
                for e in range(3):
                    lead_copy(2, e, z).wait_recv()
                square = mmt(made[1], made[1])
                lead[...] = leading[2, 0:HALF, 0:HALF] - square[0:HALF, 0:HALF]
                stage[HALF:NB, :] = leading[2, HALF:NB, :] - square[HALF:NB, :]

            @pl.when(k == 1)
            def _():
                give_part(2)

            return carry

        lax.fori_loop(0, 2, panel, 0)

    for k in range(2):
        @pl.when(pcol == k)
        def _(k=k):
            own_rows(k).wait()

    for s in range(2):
        @pl.when(prow == s)
        def _(s=s):
            own_slab(s).wait()

    def step(tick):
        pass_rows(tick)
        pass_slab(tick)

    def early(tick, carry):
        step(tick)

        @pl.when(tick < CHUNKS)
        def _():
            own_block(tick).start()

        return carry

    def part_here(part):
        for k in range(2):
            other = (1 - core) * 2 + k

            @pl.when(other < BLOCKS[part])
            def _(k=k, other=other):
                fac_copy(fac, part, other, fac_share.at[part, k], sibling).wait_recv()

        fac_split[part, 0], fac_split[part, 1] = split(fac[part])

    def first_columns(j, carry):
        step(FIRST_WORK + j)
        tile = pl.ds(pl.multiple_of(j * NB, NB), NB)
        high, low_part = split(three(fac_split[0, 0], fac_split[0, 1], *split(slab[0, :, tile])))
        c_high[0:NB, tile] = high
        c_low[0:NB, tile] = low_part
        return carry

    def first_rows(i, carry):
        step(ROWS_WORK + i)
        block = pl.ds(pl.multiple_of(i * NB, NB), NB)
        first = three_t(*split(rows[0, block, :]), fac_split[0, 0], fac_split[0, 1])
        high, low_part = split(first)
        r_high[block, 0:NB] = high
        r_low[block, 0:NB] = low_part
        rest[block, :] = rows[1, block, :] - three_t(high, low_part, fac_split[1, 0], fac_split[1, 1])
        return carry

    lax.fori_loop(0, FIRST_WORK, early, 0)
    part_here(0)
    lax.fori_loop(0, COLUMN_BLOCKS, first_columns, 0)
    lax.fori_loop(FIRST_WORK + COLUMN_BLOCKS, ROWS_WORK, early, 0)
    part_here(1)
    lax.fori_loop(0, ROW_BLOCKS, first_rows, 0)
    part_here(2)

    for j in range(COLUMN_BLOCKS):
        tile = pl.ds(j * NB, NB)
        left = slab[1, :, tile] - three(fac_split[1, 0], fac_split[1, 1], c_high[0:NB, tile], c_low[0:NB, tile])
        high, low_part = split(three(fac_split[2, 0], fac_split[2, 1], *split(left)))
        c_high[NB:2 * NB, tile] = high
        c_low[NB:2 * NB, tile] = low_part

    def second_rows(i, carry):
        block = pl.ds(pl.multiple_of(i * 2 * NB, 2 * NB), 2 * NB)
        high, low_part = split(three_t(*split(rest[block, :]), fac_split[2, 0], fac_split[2, 1]))
        r_high[block, NB:2 * NB] = high
        r_low[block, NB:2 * NB] = low_part
        return carry

    lax.fori_loop(0, ROW_BLOCKS // 2, second_rows, 0)

    def block_here(i, carry):
        own_block(i).wait()
        return carry

    lax.fori_loop(0, CHUNKS, block_here, 0)

    for k in range(2):
        for d in range(4):
            @pl.when(gives[k][d])
            def _(k=k, d=d):
                row_copy(None, k, d, 0, ROWS).wait_send()

    for s in range(2):
        for slot, condition in enumerate((along[s], across[s])):
            @pl.when(condition)
            def _(s=s, slot=slot):
                slab_copy(None, s, slot, 0, NB).wait_send()

    for part in range(3):
        for k in range(2):
            @pl.when(core * 2 + k < BLOCKS[part])
            def _(part=part, k=k):
                each_fac(part, k, finish)

        @pl.when(is_root)
        def _(part=part):
            root_fac(part, finish)

    for n, e, to_z in leads():
        @pl.when(gives_lead[n])
        def _(n=n, e=e, to_z=to_z):
            lead_copy(n, e, to_z).wait_send()


def make_panels(matrix):
    dma = pltpu.SemaphoreType.DMA
    vmem = pl.BlockSpec(memory_space=pltpu.VMEM)
    return pl.pallas_call(
        panels_kernel,
        out_shape=(
            jax.ShapeDtypeStruct((ROWS, COLS), F32),
            jax.ShapeDtypeStruct((ROWS, 2 * NB), BF16),
            jax.ShapeDtypeStruct((ROWS, 2 * NB), BF16),
            jax.ShapeDtypeStruct((2 * NB, COLS), BF16),
            jax.ShapeDtypeStruct((2 * NB, COLS), BF16),
        ),
        in_specs=[pl.BlockSpec(memory_space=pl.ANY)],
        out_specs=(vmem, vmem, vmem, vmem, vmem),
        scratch_shapes=[
            pltpu.VMEM((2, ROWS, NB), F32),
            pltpu.VMEM((2, NB, COLS), F32),
            pltpu.VMEM((3, NB, NB), F32),
            pltpu.VMEM((3, 2, NB, NB), BF16),
            pltpu.VMEM((ROWS, NB), F32),
            pltpu.VMEM((3, NB, NB), F32),
            pltpu.VMEM((3, NB, NB), F32),
            pltpu.VMEM((NB, NB), F32),
            pltpu.VMEM((HALF, HALF), F32),
            pltpu.VMEM((2, HALF, HALF), F32),
            pltpu.VMEM((HALF, HALF), F32),
            dma((5 + CHUNKS,)),
            dma((2, 4)),
            dma((2, CHUNKS)),
            dma((2, 2)),
            dma((2, STRIPS)),
            dma((3, 2, 4)),
            dma((3, 2)),
            dma((3, 4)),
            dma((sum(BLOCKS),)),
            dma((3, 3, 4)),
            dma((3, 3)),
        ],
        compiler_params=pltpu.CompilerParams(
            collective_id=0, has_side_effects=True, vmem_limit_bytes=32 * 2**20
        ),
        cost_estimate=pl.CostEstimate(flops=2**30, bytes_accessed=2**24, transcendentals=0),
        name="panels",
    )(matrix)


def update_kernel(place, w_ref, r_high, r_low, c_high, c_low, out_ref):
    i = pl.program_id(0)
    prow, pcol = place[0], place[1]
    row_block = i * 8 + prow
    block = pl.ds(pl.multiple_of(i * NB, NB), NB)
    out_ref[...] = w_ref[block, :] - three(r_high[block, :], r_low[block, :], c_high[...], c_low[...])

    @pl.when(row_block < 2)
    def _():
        out_ref[...] = jnp.zeros((NB, COLS), F32)

    down = lax.broadcasted_iota(jnp.int32, (NB, NB), 0)
    right = lax.broadcasted_iota(jnp.int32, (NB, NB), 1)
    for k in range(2):
        @pl.when(jnp.logical_and(pcol == k, row_block >= k))
        def _(k=k):
            panel = pl.ds(k * NB, NB)
            value = r_high[block, panel].astype(F32) + r_low[block, panel].astype(F32)
            keep = jnp.logical_or(row_block > k, right <= down)
            out_ref[:, 0:NB] = jnp.where(keep, value, 0.0)


def update(matrix, *panels):
    place = jnp.stack([lax.axis_index("prow"), lax.axis_index("pcol")]).astype(jnp.int32)
    vmem = pl.BlockSpec(memory_space=pltpu.VMEM)
    return pl.pallas_call(
        update_kernel,
        out_shape=jax.ShapeDtypeStruct((ROWS, COLS), F32),
        grid=(ROWS // NB,),
        in_specs=[pl.BlockSpec(memory_space=pltpu.SMEM)] + [vmem] * 5,
        out_specs=pl.BlockSpec((NB, COLS), lambda i: (i, 0)),
        compiler_params=pltpu.CompilerParams(vmem_limit_bytes=32 * 2**20),
        cost_estimate=pl.CostEstimate(
            flops=2 * 3 * ROWS * COLS * 2 * NB, bytes_accessed=2**24, transcendentals=0
        ),
        name="update",
    )(place, matrix, *panels)


def body(matrix):
    return update(*make_panels(matrix))


def solution(mesh):
    spec = P("prow", "pcol")
    return jax.shard_map(body, mesh=mesh, in_specs=(spec,), out_specs=spec, check_vma=False)
```

```python
import jax
import jax.numpy as jnp
from jax import lax
from jax.experimental import pallas as pl
from jax.experimental.pallas import tpu as pltpu

P = jax.sharding.PartitionSpec
MESH = pl.DeviceIdType.MESH
HI = lax.Precision.HIGHEST
F32 = jnp.float32
BF16 = jnp.bfloat16
NB = 256
HALF = NB // 2
ROWS = 2560
COLS = 1280
CHUNK = 64
CHUNKS = ROWS // CHUNK
STRIP = 16
STRIPS = NB // STRIP
BLOCKS = (3, 4, 3)
FIRST_MESSAGE = (0, 3, 7)
PLACES = (25, 27, 42)
ITEMS = CHUNKS + len(PLACES)
LAG = 4
DEEPEST = 5
TICKS = ITEMS + LAG * DEEPEST
SLAB_TICK = 12
OWN_TICK = 44
FIRST_WORK = PLACES[1] + LAG * DEEPEST + 1
ROWS_WORK = TICKS - ROWS // NB
COLUMN_BLOCKS = COLS // NB
ROW_BLOCKS = ROWS // NB
AHEAD = 6
PUMP = 5


def mm(a, b):
    return lax.dot_general(a, b, (((1,), (0,)), ((), ())), precision=HI, preferred_element_type=F32)


def mmt(a, b):
    return lax.dot_general(a, b, (((1,), (1,)), ((), ())), precision=HI, preferred_element_type=F32)


def split(v):
    high = v.astype(BF16)
    return high, (v - high.astype(F32)).astype(BF16)


def three(a_high, a_low, b_high, b_low, contract=0):
    def dot(p, q):
        return lax.dot_general(p, q, (((1,), (contract,)), ((), ())), preferred_element_type=F32)

    return dot(a_high, b_high) + dot(a_high, b_low) + dot(a_low, b_high)


def three_t(a_high, a_low, b_high, b_low):
    return three(a_high, a_low, b_high, b_low, 1)


def full(v):
    return jnp.broadcast_to(v, (8, 128))

def leaf(w, start):
    lane = lax.broadcasted_iota(jnp.int32, (8, 128), 1)
    sub = lax.broadcasted_iota(jnp.int32, (8, 128), 0)
    other = (lane < 64) if start else (lane >= 64)
    rows = [w[8 * i:8 * i + 8, :] for i in range(8)]
    out = []
    for b in range(8):
        c = start + 8 * b
        bc = {i: [full(rows[i][:, c + k:c + k + 1]) for k in range(8)] for i in range(b, 8)}
        e = {(l, k): full(bc[b][k][l:l + 1, :]) for k in range(8) for l in range(k, 8)}
        u = [full(rows[b][k:k + 1, :]) for k in range(8)]
        done = jnp.zeros((8, 128), F32)
        for k in range(8):
            inv = 1.0 / e[k, k]
            for m in range(k + 1, 8):
                t = e[m, k] * inv
                for l in range(m, 8):
                    e[l, m] = e[l, m] - t * e[l, k]
                u[m] = u[m] - t * u[k]
                for i in range(b + 1, 8):
                    bc[i][m] = bc[i][m] - t * bc[i][k]
            scaled = u[k] * inv
            for i in range(b + 1, 8):
                rows[i] = rows[i] - bc[i][k] * scaled
            done = jnp.where(sub == k, u[k] * lax.rsqrt(e[k, k]), done)
        out.append(jnp.where(other, done, 0.0))
    return jnp.concatenate(out, axis=0)


def chol128(s, pump):
    r = lax.broadcasted_iota(jnp.int32, (64, 128), 0)
    c = lax.broadcasted_iota(jnp.int32, (64, 128), 1)
    low = jnp.where(c == r, 1.0, 0.0)
    high = jnp.where(c == r + 64, 1.0, 0.0)
    first = leaf(jnp.where(c < 64, s[:64], high), 0)
    pump(0)
    ma = pltpu.roll(first, 64, 1)
    l21 = mmt(jnp.where(c < 64, s[64:], 0.0), ma)
    s22 = mmt(l21, l21)
    z = jnp.zeros((64, 64), F32)
    s22 = jnp.concatenate([z, s22], axis=1)
    t = mm(l21, ma)
    second = leaf(jnp.where(c < 64, low, s[64:] - s22), 64)
    pump(1)
    low_part = mm(second[:, :64], high - t)
    return jnp.concatenate([ma, low_part], axis=0)


PARENTS = (
    (
        (-1, 0, 3, 0, 8, 9, 10, 11, 12, 8, 14, 8, 0, 12, 15, 12),
        (1, -1, 14, 15, 5, 1, 5, 6, 9, 13, 9, 15, 13, 1, 13, 14),
    ),
    (
        (-1, 5, 6, 7, 0, 4, 7, 4, 4, 5, 11, 7, 8, 9, 10, 11),
        (3, -1, 1, 2, 7, 6, 2, 3, 11, 10, 6, 10, 15, 14, 2, 3),
    ),
)


def neighbour(chip, direction):
    y, x = chip // 4, chip % 4
    if direction < 2:
        return y * 4 + (x + (1, 3)[direction]) % 4
    return (y + (1, 3)[direction - 2]) % 4 * 4 + x


def depth(core, panel, chip):
    parent = PARENTS[core][panel][chip]
    return 0 if parent < 0 else 1 + depth(core, panel, parent)


def handled_at(core, panel, chip):
    return depth(core, panel, chip) if chip in PARENTS[core][panel] else DEEPEST


def senders(core, panel, direction):
    parents = PARENTS[core][panel]
    return [n for n in range(16) if parents[neighbour(n, direction)] == n]


def panels_kernel(
    a_ref, w_ref, r_high, r_low, c_high, c_low, rows, slab, fac, fac_split, rest, left, leading, made, stage, lead, inv, low,
    local_sem, row_send, row_recv, slab_send, slab_recv,
    fac_send, fac_share, fac_give, fac_recv, lead_send, lead_recv,
):
    prow, pcol = lax.axis_index("prow"), lax.axis_index("pcol")
    z, core = prow // 2, prow % 2
    y, x = pcol // 4, pcol % 4
    both = jnp.logical_and
    is_root = both(core == 1, pcol == 0)
    gives_lead = (both(prow == 0, pcol == 0), both(prow == 1, pcol == 0), both(prow == 1, pcol == 1))

    def device(pz, pc, py, px):
        return {"prow": pz * 2 + pc, "pcol": py * 4 + px}

    def on_line(axis, step):
        if axis == "x":
            return device(z, core, y, (x + step) % 4)
        if axis == "y":
            return device(z, core, (y + step) % 4, x)
        return device((z + step) % 4, core, y, x)

    sibling = device(z, 1 - core, y, x)
    root = {"prow": z * 2 + 1, "pcol": 0}

    def own_block():
        return pltpu.make_async_copy(a_ref, w_ref, local_sem.at[5])

    barrier = pltpu.get_barrier_semaphore()

    def greet(target):
        pl.semaphore_signal(barrier, 1, device_id=target, device_id_type=MESH)

    for axis in "xyz":
        for step in (1, 2, 3):
            greet(on_line(axis, step))
    greet(sibling)

    @pl.when(both(is_root, z > 0))
    def _():
        greet({"prow": 0, "pcol": 0})
        greet({"prow": 1, "pcol": 1})

    @pl.when(both(core == 0, pcol == 1))
    def _():
        greet(root)

    extra = jnp.where(is_root, 1, 0) + jnp.where(jnp.logical_or(gives_lead[0], gives_lead[2]), 3, 0)
    pl.semaphore_wait(barrier, 10 + extra)

    index = core * 16 + pcol
    gives = [[None] * 4 for _ in range(2)]
    for k in range(2):
        for d in range(4):
            flag = jnp.int32(0)
            for c in range(2):
                for n in senders(c, k, d):
                    flag = flag + jnp.where(index == c * 16 + n, 1, 0)
            gives[k][d] = flag == 1
    depths = []
    for k in range(2):
        value = jnp.int32(0)
        for c in range(2):
            for n in range(16):
                value = value + jnp.where(index == c * 16 + n, handled_at(c, k, n), 0)
        depths.append(value)
    targets = (on_line("x", 1), on_line("x", 3), on_line("y", 1), on_line("y", 3))

    def row_copy(src, k, d, first, count):
        piece = pl.ds(first, count)
        return pltpu.make_async_remote_copy(
            src_ref=src.at[piece, pl.ds(0, NB)] if src is a_ref else rows.at[k, piece, :],
            dst_ref=rows.at[k, piece, :],
            send_sem=row_send.at[k, d],
            recv_sem=row_recv.at[k, first // CHUNK if count == CHUNK else 0],
            device_id=targets[d],
            device_id_type=MESH,
        )

    on_ring = (core == 0, core == jnp.where(pcol == 0, 0, 1))
    along = (both(on_ring[0], z < 3), both(on_ring[1], z != 1))
    start_of_one = both(pcol == 0, z == 0)
    across = (on_ring[0], jnp.logical_or(both(start_of_one, core == 1), both(on_ring[1], jnp.logical_not(start_of_one))))
    slab_depths = (
        z + jnp.where(on_ring[0], 0, 1),
        (4 - z) % 4 + jnp.where(on_ring[1], 0, 1) + jnp.where(pcol == 0, 1, 0),
    )

    def slab_copy(src, s, slot, first, count):
        piece = pl.ds(first, count)
        step = 1 if s == 0 else 3
        return pltpu.make_async_remote_copy(
            src_ref=a_ref.at[piece, :] if src is a_ref else slab.at[s, piece, :],
            dst_ref=slab.at[s, piece, :],
            send_sem=slab_send.at[s, slot],
            recv_sem=slab_recv.at[s, first // STRIP if count == STRIP else 0],
            device_id=on_line("z", step) if slot == 0 else sibling,
            device_id_type=MESH,
        )

    def own_rows(k):
        return pltpu.make_async_copy(a_ref.at[:, pl.ds(0, NB)], rows.at[k], local_sem.at[k])

    def own_slab(s):
        return pltpu.make_async_copy(a_ref.at[pl.ds(0, NB), :], slab.at[s], local_sem.at[2 + s])

    def own_lead():
        return pltpu.make_async_copy(a_ref.at[pl.ds(0, NB), pl.ds(0, NB)], leading.at[1], local_sem.at[4])

    def lead_copy(n, e, to_z):
        down, right, size = (0, 0, NB) if n == 1 else ((e + 1) // 2 * HALF, e // 2 * HALF, HALF)
        return pltpu.make_async_remote_copy(
            src_ref=a_ref.at[pl.ds(down, size), pl.ds(right, size)],
            dst_ref=leading.at[n, pl.ds(down, size), pl.ds(right, size)],
            send_sem=lead_send.at[n, e, to_z],
            recv_sem=lead_recv.at[n, e],
            device_id={"prow": 2 * to_z + 1, "pcol": 0},
            device_id_type=MESH,
        )

    def leads():
        for n in range(3):
            for e in range(1 if n == 1 else 3):
                for to_z in ((1, 3, 2) if n == 1 else (0, 1, 3, 2)):
                    yield n, e, to_z

    for n, e, to_z in leads():
        @pl.when(gives_lead[n])
        def _(n=n, e=e, to_z=to_z):
            lead_copy(n, e, to_z).start()

    @pl.when(gives_lead[1])
    def _():
        own_lead().start()

    for s in range(2):
        @pl.when(prow == s)
        def _(s=s):
            own_slab(s).start()

    for k in range(2):
        @pl.when(pcol == k)
        def _(k=k):
            own_rows(k).start()

    def send_chunk(src, k, i):
        for d in range(4):
            @pl.when(gives[k][d])
            def _(d=d):
                row_copy(src, k, d, i * CHUNK, CHUNK).start()

    def send_strip(src, s, j):
        @pl.when(along[s])
        def _():
            slab_copy(src, s, 0, j * STRIP, STRIP).start()

        @pl.when(across[s])
        def _():
            slab_copy(src, s, 1, j * STRIP, STRIP).start()

    def fac_block(ref, part, e):
        i, j = (e // 2, e % 2) if part == 1 else ((e + 1) // 2, e // 2)
        if not isinstance(e, int):
            i, j = pl.multiple_of(i * HALF, HALF), pl.multiple_of(j * HALF, HALF)
        else:
            i, j = i * HALF, j * HALF
        return ref.at[part, pl.ds(i, HALF), pl.ds(j, HALF)]

    def fac_copy(src, part, e, send_sem, target):
        return pltpu.make_async_remote_copy(
            src_ref=fac_block(src, part, e),
            dst_ref=fac_block(fac, part, e),
            send_sem=send_sem,
            recv_sem=fac_recv.at[FIRST_MESSAGE[part] + e],
            device_id=target,
            device_id_type=MESH,
        )

    def each_fac(part, k, act):
        e = core * 2 + k
        for d in range(4):
            @pl.when(gives[k][d])
            def _(d=d):
                act(fac_copy(fac, part, e, fac_send.at[part, k, d], targets[d]))
        act(fac_copy(fac, part, e, fac_share.at[part, k], sibling))

    def root_fac(part, act):
        for e, target in ((0, sibling), (1, {"prow": z * 2, "pcol": 1}), (3, {"prow": z * 2 + 1, "pcol": 1})):
            if e < BLOCKS[part]:
                act(fac_copy(made, part, e, fac_give.at[part, e], target))

    def begin(copy):
        copy.start()

    def finish(copy):
        copy.wait_send()

    def give_part(part):
        root_fac(part, begin)
        i, j = (1, 0) if part == 1 else (1, 1)
        span = (part, pl.ds(i * HALF, HALF), pl.ds(j * HALF, HALF))
        fac[span] = made[span]
        each_fac(part, 0, begin)

    def pass_rows(tick):
        for k in range(2):
            n = tick - LAG * depths[k]
            skips = jnp.int32(0)
            special = n < 0
            for place in PLACES:
                skips = skips + jnp.where(n > place, 1, 0)
                special = jnp.logical_or(special, n == place)
            i = n - skips
            here = both(jnp.logical_not(special), n < ITEMS)
            mine = both(here, pcol == k)
            if k == 0:
                mine = both(mine, jnp.logical_not(is_root))

            @pl.when(both(here, pcol != k))
            def _(k=k, i=i):
                row_copy(None, k, 0, i * CHUNK, CHUNK).wait_recv()
                send_chunk(None, k, i)

            @pl.when(mine)
            def _(k=k, i=i):
                send_chunk(a_ref, k, i)

            for part, place in enumerate(PLACES):
                now = both(n == place, core * 2 + k < BLOCKS[part])
                if k == 0:
                    now = both(now, jnp.logical_not(is_root))

                @pl.when(now)
                def _(k=k, part=part):
                    fac_copy(fac, part, core * 2 + k, fac_share.at[part, k], sibling).wait_recv()
                    each_fac(part, k, begin)

    def pass_slab(tick):
        for s in range(2):
            j = tick - SLAB_TICK - LAG * slab_depths[s]
            here = both(j >= 0, j < STRIPS)

            @pl.when(both(here, prow != s))
            def _(s=s, j=j):
                slab_copy(None, s, 0, j * STRIP, STRIP).wait_recv()
                send_strip(None, s, j)

            @pl.when(both(both(tick < STRIPS, prow == s), jnp.logical_not(is_root)))
            def _(s=s):
                send_strip(a_ref, s, tick)

    for part in (0, 2):
        fac[part, 0:HALF, HALF:NB] = jnp.zeros((HALF, HALF), F32)

    @pl.when(is_root)
    def _():
        def pump(first, count):
            def one(i, carry):
                @pl.when(i < CHUNKS)
                def _():
                    send_chunk(a_ref, 0, i)

                return carry

            lax.fori_loop(first, first + count, one, 0)

        pump(0, AHEAD)

        @pl.when(prow == 1)
        def _():
            def one(j, carry):
                send_strip(a_ref, 1, j)
                return carry

            lax.fori_loop(0, STRIPS, one, 0)

        lead_copy(0, 0, z).wait_recv()
        lead[...] = leading[0, 0:HALF, 0:HALF]

        def panel(k, carry):
            def half(h, inner):
                inv[h] = chol128(lead[...], lambda n: pump(AHEAD + (4 * k + 2 * h + n) * PUMP, PUMP))

                @pl.when(h == 0)
                def _():
                    @pl.when(k == 0)
                    def _():
                        for e in (1, 2):
                            lead_copy(0, e, z).wait_recv()
                        stage[...] = leading[0, HALF:NB, :]

                    @pl.when(k == 1)
                    def _():
                        for e in (1, 2):
                            lead_copy(2, e, z).wait_recv()
                        stage[...] = leading[2, HALF:NB, :] - mmt(made[1, HALF:NB, :], made[1])

                    low[...] = mmt(stage[:, 0:HALF], inv[0])
                    lead[...] = stage[:, HALF:NB] - mmt(low[...], low[...])

                return inner

            lax.fori_loop(0, 2, half, 0)
            made[2 * k, 0:HALF, 0:HALF] = inv[0]
            made[2 * k, 0:HALF, HALF:NB] = jnp.zeros((HALF, HALF), F32)
            made[2 * k, HALF:NB, HALF:NB] = inv[1]
            made[2 * k, HALF:NB, 0:HALF] = -mm(inv[1], mm(low[...], inv[0]))

            @pl.when(k == 0)
            def _():
                give_part(0)

                @pl.when(prow == 1)
                def _():
                    own_lead().wait()

                @pl.when(prow != 1)
                def _():
                    lead_copy(1, 0, z).wait_recv()

                made[1] = mmt(leading[1], made[0])
                lead_copy(2, 0, z).wait_recv()
                top = made[1, 0:HALF, :]
                lead[...] = leading[2, 0:HALF, 0:HALF] - mmt(top, top)
                give_part(1)

            @pl.when(k == 1)
            def _():
                give_part(2)

            return carry

        lax.fori_loop(0, 2, panel, 0)

    for k in range(2):
        @pl.when(pcol == k)
        def _(k=k):
            own_rows(k).wait()

    for s in range(2):
        @pl.when(prow == s)
        def _(s=s):
            own_slab(s).wait()

    def step(tick):
        pass_rows(tick)
        pass_slab(tick)

    def early(tick, carry):
        step(tick)

        @pl.when(tick == OWN_TICK)
        def _():
            own_block().start()

        return carry

    def part_here(part):
        for k in range(2):
            other = (1 - core) * 2 + k

            @pl.when(other < BLOCKS[part])
            def _(k=k, other=other):
                fac_copy(fac, part, other, fac_share.at[part, k], sibling).wait_recv()

        fac_split[part, 0], fac_split[part, 1] = split(fac[part])

    def first_columns(j, carry):
        step(FIRST_WORK + j)
        tile = pl.ds(pl.multiple_of(j * NB, NB), NB)
        high, low_part = split(three(fac_split[0, 0], fac_split[0, 1], *split(slab[0, :, tile])))
        c_high[0:NB, tile] = high
        c_low[0:NB, tile] = low_part
        left[:, tile] = slab[1, :, tile] - three(fac_split[1, 0], fac_split[1, 1], high, low_part)
        return carry

    def first_rows(i, carry):
        step(ROWS_WORK + i)
        block = pl.ds(pl.multiple_of(i * NB, NB), NB)
        first = three_t(*split(rows[0, block, :]), fac_split[0, 0], fac_split[0, 1])
        high, low_part = split(first)
        r_high[block, 0:NB] = high
        r_low[block, 0:NB] = low_part
        rest[block, :] = rows[1, block, :] - three_t(high, low_part, fac_split[1, 0], fac_split[1, 1])
        return carry

    @pl.when(jnp.logical_not(is_root))
    def _():
        lax.fori_loop(0, FIRST_WORK, early, 0)

    @pl.when(is_root)
    def _():
        own_block().start()

        def chunk_here(i, carry):
            row_copy(None, 1, 0, i * CHUNK, CHUNK).wait_recv()
            return carry

        first_ticks = FIRST_WORK - LAG * DEEPEST
        lax.fori_loop(0, first_ticks - sum(place < first_ticks for place in PLACES), chunk_here, 0)
        fac_copy(fac, 1, 3, fac_share.at[1, 1], sibling).wait_recv()
        each_fac(1, 1, begin)

        for s in range(2):
            @pl.when(prow != s)
            def _(s=s):
                def strip_here(j, carry):
                    slab_copy(None, s, 0, j * STRIP, STRIP).wait_recv()
                    return carry

                lax.fori_loop(0, STRIPS, strip_here, 0)

    part_here(0)
    part_here(1)
    lax.fori_loop(0, COLUMN_BLOCKS, first_columns, 0)
    lax.fori_loop(FIRST_WORK + COLUMN_BLOCKS, ROWS_WORK, early, 0)
    lax.fori_loop(0, ROW_BLOCKS, first_rows, 0)
    part_here(2)

    for j in range(COLUMN_BLOCKS):
        tile = pl.ds(j * NB, NB)
        high, low_part = split(three(fac_split[2, 0], fac_split[2, 1], *split(left[:, tile])))
        c_high[NB:2 * NB, tile] = high
        c_low[NB:2 * NB, tile] = low_part

    def second_rows(i, carry):
        block = pl.ds(pl.multiple_of(i * 2 * NB, 2 * NB), 2 * NB)
        high, low_part = split(three_t(*split(rest[block, :]), fac_split[2, 0], fac_split[2, 1]))
        r_high[block, NB:2 * NB] = high
        r_low[block, NB:2 * NB] = low_part
        return carry

    lax.fori_loop(0, ROW_BLOCKS // 2, second_rows, 0)

    own_block().wait()

    for k in range(2):
        for d in range(4):
            @pl.when(gives[k][d])
            def _(k=k, d=d):
                row_copy(None, k, d, 0, ROWS).wait_send()

    for s in range(2):
        for slot, condition in enumerate((along[s], across[s])):
            @pl.when(condition)
            def _(s=s, slot=slot):
                slab_copy(None, s, slot, 0, NB).wait_send()

    for part in range(3):
        for k in range(2):
            @pl.when(core * 2 + k < BLOCKS[part])
            def _(part=part, k=k):
                each_fac(part, k, finish)

        @pl.when(is_root)
        def _(part=part):
            root_fac(part, finish)

    for n, e, to_z in leads():
        @pl.when(gives_lead[n])
        def _(n=n, e=e, to_z=to_z):
            lead_copy(n, e, to_z).wait_send()


def make_panels(matrix):
    dma = pltpu.SemaphoreType.DMA
    vmem = pl.BlockSpec(memory_space=pltpu.VMEM)
    return pl.pallas_call(
        panels_kernel,
        out_shape=(
            jax.ShapeDtypeStruct((ROWS, COLS), F32),
            jax.ShapeDtypeStruct((ROWS, 2 * NB), BF16),
            jax.ShapeDtypeStruct((ROWS, 2 * NB), BF16),
            jax.ShapeDtypeStruct((2 * NB, COLS), BF16),
            jax.ShapeDtypeStruct((2 * NB, COLS), BF16),
        ),
        in_specs=[pl.BlockSpec(memory_space=pl.ANY)],
        out_specs=(vmem, vmem, vmem, vmem, vmem),
        scratch_shapes=[
            pltpu.VMEM((2, ROWS, NB), F32),
            pltpu.VMEM((2, NB, COLS), F32),
            pltpu.VMEM((3, NB, NB), F32),
            pltpu.VMEM((3, 2, NB, NB), BF16),
            pltpu.VMEM((ROWS, NB), F32),
            pltpu.VMEM((NB, COLS), F32),
            pltpu.VMEM((3, NB, NB), F32),
            pltpu.VMEM((3, NB, NB), F32),
            pltpu.VMEM((HALF, NB), F32),
            pltpu.VMEM((HALF, HALF), F32),
            pltpu.VMEM((2, HALF, HALF), F32),
            pltpu.VMEM((HALF, HALF), F32),
            dma((6,)),
            dma((2, 4)),
            dma((2, CHUNKS)),
            dma((2, 2)),
            dma((2, STRIPS)),
            dma((3, 2, 4)),
            dma((3, 2)),
            dma((3, 4)),
            dma((sum(BLOCKS),)),
            dma((3, 3, 4)),
            dma((3, 3)),
        ],
        compiler_params=pltpu.CompilerParams(
            collective_id=0, has_side_effects=True, vmem_limit_bytes=32 * 2**20
        ),
        cost_estimate=pl.CostEstimate(flops=2**30, bytes_accessed=2**24, transcendentals=0),
        name="panels",
    )(matrix)


def update_kernel(w_ref, r_high, r_low, c_high, c_low, out_ref):
    i = pl.program_id(0)
    prow, pcol = lax.axis_index("prow"), lax.axis_index("pcol")
    row_block = i * 8 + prow
    block = pl.ds(pl.multiple_of(i * NB, NB), NB)
    out_ref[...] = w_ref[block, :] - three(r_high[block, :], r_low[block, :], c_high[...], c_low[...])

    @pl.when(row_block < 2)
    def _():
        out_ref[...] = jnp.zeros((NB, COLS), F32)

    down = lax.broadcasted_iota(jnp.int32, (NB, NB), 0)
    right = lax.broadcasted_iota(jnp.int32, (NB, NB), 1)
    for k in range(2):
        @pl.when(jnp.logical_and(pcol == k, row_block >= k))
        def _(k=k):
            panel = pl.ds(k * NB, NB)
            value = r_high[block, panel].astype(F32) + r_low[block, panel].astype(F32)
            keep = jnp.logical_or(row_block > k, right <= down)
            out_ref[:, 0:NB] = jnp.where(keep, value, 0.0)


def update(matrix, *panels):
    vmem = pl.BlockSpec(memory_space=pltpu.VMEM)
    return pl.pallas_call(
        update_kernel,
        out_shape=jax.ShapeDtypeStruct((ROWS, COLS), F32),
        grid=(ROWS // NB,),
        in_specs=[vmem] * 5,
        out_specs=pl.BlockSpec((NB, COLS), lambda i: (i, 0)),
        compiler_params=pltpu.CompilerParams(vmem_limit_bytes=32 * 2**20),
        cost_estimate=pl.CostEstimate(
            flops=2 * 3 * ROWS * COLS * 2 * NB, bytes_accessed=2**24, transcendentals=0
        ),
        name="update",
    )(matrix, *panels)


def body(matrix):
    return update(*make_panels(matrix))


def solution(mesh):
    spec = P("prow", "pcol")
    return jax.shard_map(body, mesh=mesh, in_specs=(spec,), out_specs=spec, check_vma=False)
```

```python
import jax
import jax.numpy as jnp
from jax import lax
from jax.experimental import pallas as pl
from jax.experimental.pallas import tpu as pltpu

P = jax.sharding.PartitionSpec
MESH = pl.DeviceIdType.MESH
HI = lax.Precision.HIGHEST
F32 = jnp.float32
BF16 = jnp.bfloat16
NB = 256
HALF = NB // 2
ROWS = 2560
COLS = 1280
CHUNK = 64
CHUNKS = ROWS // CHUNK
STRIP = 16
STRIPS = NB // STRIP
BLOCKS = (3, 4, 3)
FIRST_MESSAGE = (0, 3, 7)
PLACES = (25, 27, 40)
ITEMS = CHUNKS + len(PLACES)
LAG = 4
DEEPEST = 5
TICKS = ITEMS + LAG * DEEPEST
SLAB_TICK = 12
OWN_TICK = 44
FIRST_WORK = PLACES[1] + LAG * DEEPEST + 1
ROWS_WORK = TICKS - ROWS // NB
COLUMN_BLOCKS = COLS // NB
ROW_BLOCKS = ROWS // NB
AHEAD = 6
PUMP = 5


def mm(a, b):
    return lax.dot_general(a, b, (((1,), (0,)), ((), ())), precision=HI, preferred_element_type=F32)


def mmt(a, b):
    return lax.dot_general(a, b, (((1,), (1,)), ((), ())), precision=HI, preferred_element_type=F32)


def split(v):
    high = v.astype(BF16)
    return high, (v - high.astype(F32)).astype(BF16)


def three(a_high, a_low, b_high, b_low, contract=0):
    def dot(p, q):
        return lax.dot_general(p, q, (((1,), (contract,)), ((), ())), preferred_element_type=F32)

    return dot(a_high, b_high) + dot(a_high, b_low) + dot(a_low, b_high)


def three_t(a_high, a_low, b_high, b_low):
    return three(a_high, a_low, b_high, b_low, 1)


def full(v):
    return jnp.broadcast_to(v, (8, 128))

def leaf(w, start):
    lane = lax.broadcasted_iota(jnp.int32, (8, 128), 1)
    sub = lax.broadcasted_iota(jnp.int32, (8, 128), 0)
    other = (lane < 64) if start else (lane >= 64)
    rows = [w[8 * i:8 * i + 8, :] for i in range(8)]
    out = []
    for b in range(8):
        c = start + 8 * b
        bc = {i: [full(rows[i][:, c + k:c + k + 1]) for k in range(8)] for i in range(b, 8)}
        e = {(l, k): full(bc[b][k][l:l + 1, :]) for k in range(8) for l in range(k, 8)}
        u = [full(rows[b][k:k + 1, :]) for k in range(8)]
        done = jnp.zeros((8, 128), F32)
        for k in range(8):
            inv = 1.0 / e[k, k]
            for m in range(k + 1, 8):
                t = e[m, k] * inv
                for l in range(m, 8):
                    e[l, m] = e[l, m] - t * e[l, k]
                u[m] = u[m] - t * u[k]
                for i in range(b + 1, 8):
                    bc[i][m] = bc[i][m] - t * bc[i][k]
            scaled = u[k] * inv
            for i in range(b + 1, 8):
                rows[i] = rows[i] - bc[i][k] * scaled
            done = jnp.where(sub == k, u[k] * lax.rsqrt(e[k, k]), done)
        out.append(jnp.where(other, done, 0.0))
    return jnp.concatenate(out, axis=0)


def chol128(s, pump):
    r = lax.broadcasted_iota(jnp.int32, (64, 128), 0)
    c = lax.broadcasted_iota(jnp.int32, (64, 128), 1)
    low = jnp.where(c == r, 1.0, 0.0)
    high = jnp.where(c == r + 64, 1.0, 0.0)
    first = leaf(jnp.where(c < 64, s[:64], high), 0)
    pump(0)
    ma = pltpu.roll(first, 64, 1)
    l21 = mmt(jnp.where(c < 64, s[64:], 0.0), ma)
    s22 = mmt(l21, l21)
    z = jnp.zeros((64, 64), F32)
    s22 = jnp.concatenate([z, s22], axis=1)
    t = mm(l21, ma)
    second = leaf(jnp.where(c < 64, low, s[64:] - s22), 64)
    pump(1)
    low_part = mm(second[:, :64], high - t)
    return jnp.concatenate([ma, low_part], axis=0)


PARENTS = (
    (
        (-1, 0, 3, 0, 8, 9, 10, 11, 12, 8, 14, 8, 0, 12, 15, 12),
        (1, -1, 14, 15, 5, 1, 5, 6, 9, 13, 9, 15, 13, 1, 13, 14),
    ),
    (
        (-1, 5, 6, 7, 0, 4, 7, 4, 4, 5, 11, 7, 8, 9, 10, 11),
        (3, -1, 1, 2, 7, 6, 2, 3, 11, 10, 6, 10, 15, 14, 2, 3),
    ),
)


def neighbour(chip, direction):
    y, x = chip // 4, chip % 4
    if direction < 2:
        return y * 4 + (x + (1, 3)[direction]) % 4
    return (y + (1, 3)[direction - 2]) % 4 * 4 + x


def depth(core, panel, chip):
    parent = PARENTS[core][panel][chip]
    return 0 if parent < 0 else 1 + depth(core, panel, parent)


def handled_at(core, panel, chip):
    return depth(core, panel, chip) if chip in PARENTS[core][panel] else DEEPEST


def senders(core, panel, direction):
    parents = PARENTS[core][panel]
    return [n for n in range(16) if parents[neighbour(n, direction)] == n]


(ROOT_GIVES,) = [d for d in range(4) if 0 in senders(1, 0, d)]


def panels_kernel(
    a_ref, w_ref, r_high, r_low, c_high, c_low, rows, slab, fac, fac_split, rest, left, leading, made, stage, lead, inv, low,
    local_sem, row_send, row_recv, slab_send, slab_recv,
    fac_send, fac_share, fac_give, fac_recv, lead_send, lead_recv,
):
    prow, pcol = lax.axis_index("prow"), lax.axis_index("pcol")
    z, core = prow // 2, prow % 2
    y, x = pcol // 4, pcol % 4
    both = jnp.logical_and
    is_root = both(core == 1, pcol == 0)
    gives_lead = (both(prow == 0, pcol == 0), both(prow == 1, pcol == 0), both(prow == 1, pcol == 1))

    def device(pz, pc, py, px):
        return {"prow": pz * 2 + pc, "pcol": py * 4 + px}

    def on_line(axis, step):
        if axis == "x":
            return device(z, core, y, (x + step) % 4)
        if axis == "y":
            return device(z, core, (y + step) % 4, x)
        return device((z + step) % 4, core, y, x)

    sibling = device(z, 1 - core, y, x)
    root = {"prow": z * 2 + 1, "pcol": 0}

    def own_block():
        return pltpu.make_async_copy(a_ref, w_ref, local_sem.at[5])

    barrier = pltpu.get_barrier_semaphore()

    def greet(target):
        pl.semaphore_signal(barrier, 1, device_id=target, device_id_type=MESH)

    for axis, steps in (("x", (1, 3)), ("y", (1, 3)), ("z", (1, 2, 3))):
        for step in steps:
            greet(on_line(axis, step))
    greet(sibling)

    @pl.when(both(is_root, z > 0))
    def _():
        greet({"prow": 0, "pcol": 0})
        greet({"prow": 1, "pcol": 1})

    @pl.when(both(core == 0, pcol == 1))
    def _():
        greet(root)

    extra = jnp.where(is_root, 1, 0) + jnp.where(jnp.logical_or(gives_lead[0], gives_lead[2]), 3, 0)
    index = core * 16 + pcol
    gives = [[None] * 4 for _ in range(2)]
    for k in range(2):
        for d in range(4):
            flag = jnp.int32(0)
            for c in range(2):
                for n in senders(c, k, d):
                    flag = flag + jnp.where(index == c * 16 + n, 1, 0)
            gives[k][d] = flag == 1
    depths = []
    for k in range(2):
        value = jnp.int32(0)
        for c in range(2):
            for n in range(16):
                value = value + jnp.where(index == c * 16 + n, handled_at(c, k, n), 0)
        depths.append(value)
    pl.semaphore_wait(barrier, 8 + extra)
    targets = (on_line("x", 1), on_line("x", 3), on_line("y", 1), on_line("y", 3))

    def row_copy(src, k, d, first, count):
        piece = pl.ds(first, count)
        return pltpu.make_async_remote_copy(
            src_ref=src.at[piece, pl.ds(0, NB)] if src is a_ref else rows.at[k, piece, :],
            dst_ref=rows.at[k, piece, :],
            send_sem=row_send.at[k, d],
            recv_sem=row_recv.at[k, first // CHUNK if count == CHUNK else 0],
            device_id=targets[d],
            device_id_type=MESH,
        )

    on_ring = (core == 0, core == jnp.where(pcol == 0, 0, 1))
    along = (both(on_ring[0], z < 3), both(on_ring[1], z != 1))
    start_of_one = both(pcol == 0, z == 0)
    across = (on_ring[0], jnp.logical_or(both(start_of_one, core == 1), both(on_ring[1], jnp.logical_not(start_of_one))))
    slab_depths = (
        z + jnp.where(on_ring[0], 0, 1),
        (4 - z) % 4 + jnp.where(on_ring[1], 0, 1) + jnp.where(pcol == 0, 1, 0),
    )

    def slab_copy(src, s, slot, first, count):
        piece = pl.ds(first, count)
        step = 1 if s == 0 else 3
        return pltpu.make_async_remote_copy(
            src_ref=a_ref.at[piece, :] if src is a_ref else slab.at[s, piece, :],
            dst_ref=slab.at[s, piece, :],
            send_sem=slab_send.at[s, slot],
            recv_sem=slab_recv.at[s, first // STRIP if count == STRIP else 0],
            device_id=on_line("z", step) if slot == 0 else sibling,
            device_id_type=MESH,
        )

    def own_rows(k):
        return pltpu.make_async_copy(a_ref.at[:, pl.ds(0, NB)], rows.at[k], local_sem.at[k])

    def own_slab(s):
        return pltpu.make_async_copy(a_ref.at[pl.ds(0, NB), :], slab.at[s], local_sem.at[2 + s])

    def own_lead():
        return pltpu.make_async_copy(a_ref.at[pl.ds(0, NB), pl.ds(0, NB)], leading.at[1], local_sem.at[4])

    def lead_copy(n, e, to_z):
        down, right, size = (0, 0, NB) if n == 1 else ((e + 1) // 2 * HALF, e // 2 * HALF, HALF)
        return pltpu.make_async_remote_copy(
            src_ref=a_ref.at[pl.ds(down, size), pl.ds(right, size)],
            dst_ref=leading.at[n, pl.ds(down, size), pl.ds(right, size)],
            send_sem=lead_send.at[n, e, to_z],
            recv_sem=lead_recv.at[n, e],
            device_id={"prow": 2 * to_z + 1, "pcol": 0},
            device_id_type=MESH,
        )

    def leads():
        for n in range(3):
            for e in range(1 if n == 1 else 3):
                for to_z in ((1, 3, 2) if n == 1 else (0, 1, 3, 2)):
                    yield n, e, to_z

    for n, e, to_z in leads():
        @pl.when(gives_lead[n])
        def _(n=n, e=e, to_z=to_z):
            lead_copy(n, e, to_z).start()

    @pl.when(gives_lead[1])
    def _():
        own_lead().start()

    for s in range(2):
        @pl.when(prow == s)
        def _(s=s):
            own_slab(s).start()

    for k in range(2):
        @pl.when(pcol == k)
        def _(k=k):
            own_rows(k).start()

    def send_chunk(src, k, i):
        for d in range(4):
            @pl.when(gives[k][d])
            def _(d=d):
                row_copy(src, k, d, i * CHUNK, CHUNK).start()

    def send_strip(src, s, j):
        @pl.when(along[s])
        def _():
            slab_copy(src, s, 0, j * STRIP, STRIP).start()

        @pl.when(across[s])
        def _():
            slab_copy(src, s, 1, j * STRIP, STRIP).start()

    def fac_block(ref, part, e):
        i, j = (e // 2, e % 2) if part == 1 else ((e + 1) // 2, e // 2)
        if not isinstance(e, int):
            i, j = pl.multiple_of(i * HALF, HALF), pl.multiple_of(j * HALF, HALF)
        else:
            i, j = i * HALF, j * HALF
        return ref.at[part, pl.ds(i, HALF), pl.ds(j, HALF)]

    def fac_copy(src, part, e, send_sem, target):
        return pltpu.make_async_remote_copy(
            src_ref=fac_block(src, part, e),
            dst_ref=fac_block(fac, part, e),
            send_sem=send_sem,
            recv_sem=fac_recv.at[FIRST_MESSAGE[part] + e],
            device_id=target,
            device_id_type=MESH,
        )

    def each_fac(part, k, act):
        e = core * 2 + k
        for d in range(4):
            @pl.when(gives[k][d])
            def _(d=d):
                act(fac_copy(fac, part, e, fac_send.at[part, k, d], targets[d]))
        act(fac_copy(fac, part, e, fac_share.at[part, k], sibling))

    def root_fac(part, act):
        for e, target in ((0, sibling), (1, {"prow": z * 2, "pcol": 1}), (3, {"prow": z * 2 + 1, "pcol": 1})):
            if e < BLOCKS[part]:
                act(fac_copy(made, part, e, fac_give.at[part, e], target))

    def begin(copy):
        copy.start()

    def finish(copy):
        copy.wait_send()

    def give_part(part):
        root_fac(part, begin)
        i, j = (1, 0) if part == 1 else (1, 1)
        span = (part, pl.ds(i * HALF, HALF), pl.ds(j * HALF, HALF))
        fac[span] = made[span]
        each_fac(part, 0, begin)

    def pass_rows(tick):
        for k in range(2):
            n = tick - LAG * depths[k]
            skips = jnp.int32(0)
            special = n < 0
            for place in PLACES:
                skips = skips + jnp.where(n > place, 1, 0)
                special = jnp.logical_or(special, n == place)
            i = n - skips
            here = both(jnp.logical_not(special), n < ITEMS)
            mine = both(here, pcol == k)
            if k == 0:
                mine = both(mine, jnp.logical_not(is_root))

            @pl.when(both(here, pcol != k))
            def _(k=k, i=i):
                row_copy(None, k, 0, i * CHUNK, CHUNK).wait_recv()
                send_chunk(None, k, i)

            @pl.when(mine)
            def _(k=k, i=i):
                send_chunk(a_ref, k, i)

            for part, place in enumerate(PLACES):
                now = both(n == place, core * 2 + k < BLOCKS[part])
                if k == 0:
                    now = both(now, jnp.logical_not(is_root))

                @pl.when(now)
                def _(k=k, part=part):
                    fac_copy(fac, part, core * 2 + k, fac_share.at[part, k], sibling).wait_recv()
                    each_fac(part, k, begin)

    def pass_slab(tick):
        for s in range(2):
            j = tick - SLAB_TICK - LAG * slab_depths[s]
            here = both(j >= 0, j < STRIPS)

            @pl.when(both(here, prow != s))
            def _(s=s, j=j):
                slab_copy(None, s, 0, j * STRIP, STRIP).wait_recv()
                send_strip(None, s, j)

            @pl.when(both(both(tick < STRIPS, prow == s), jnp.logical_not(is_root)))
            def _(s=s):
                send_strip(a_ref, s, tick)

    for part in (0, 2):
        fac[part, 0:HALF, HALF:NB] = jnp.zeros((HALF, HALF), F32)

    @pl.when(is_root)
    def _():
        def pump(first, count):
            def one(i, carry):
                @pl.when(i < CHUNKS)
                def _():
                    row_copy(a_ref, 0, ROOT_GIVES, i * CHUNK, CHUNK).start()

                return carry

            lax.fori_loop(first, first + count, one, 0)

        pump(0, AHEAD)

        @pl.when(prow == 1)
        def _():
            def one(j, carry):
                send_strip(a_ref, 1, j)
                return carry

            lax.fori_loop(0, STRIPS, one, 0)

        lead_copy(0, 0, z).wait_recv()
        lead[...] = leading[0, 0:HALF, 0:HALF]

        def panel(k, carry):
            def half(h, inner):
                inv[h] = chol128(lead[...], lambda n: pump(AHEAD + (4 * k + 2 * h + n) * PUMP, PUMP))

                @pl.when(h == 0)
                def _():
                    @pl.when(k == 0)
                    def _():
                        for e in (1, 2):
                            lead_copy(0, e, z).wait_recv()
                        stage[...] = leading[0, HALF:NB, :]

                    @pl.when(k == 1)
                    def _():
                        for e in (1, 2):
                            lead_copy(2, e, z).wait_recv()
                        stage[...] = leading[2, HALF:NB, :] - mmt(made[1, HALF:NB, :], made[1])

                    low[...] = mmt(stage[:, 0:HALF], inv[0])
                    lead[...] = stage[:, HALF:NB] - mmt(low[...], low[...])

                return inner

            lax.fori_loop(0, 2, half, 0)
            made[2 * k, 0:HALF, 0:HALF] = inv[0]
            made[2 * k, 0:HALF, HALF:NB] = jnp.zeros((HALF, HALF), F32)
            made[2 * k, HALF:NB, HALF:NB] = inv[1]
            made[2 * k, HALF:NB, 0:HALF] = -mm(inv[1], mm(low[...], inv[0]))

            @pl.when(k == 0)
            def _():
                give_part(0)

                @pl.when(prow == 1)
                def _():
                    own_lead().wait()

                @pl.when(prow != 1)
                def _():
                    lead_copy(1, 0, z).wait_recv()

                made[1] = mmt(leading[1], made[0])
                lead_copy(2, 0, z).wait_recv()
                top = made[1, 0:HALF, :]
                lead[...] = leading[2, 0:HALF, 0:HALF] - mmt(top, top)
                give_part(1)

            @pl.when(k == 1)
            def _():
                give_part(2)

            return carry

        lax.fori_loop(0, 2, panel, 0)

    for k in range(2):
        @pl.when(pcol == k)
        def _(k=k):
            own_rows(k).wait()

    for s in range(2):
        @pl.when(prow == s)
        def _(s=s):
            own_slab(s).wait()

    def step(tick):
        pass_rows(tick)
        pass_slab(tick)

    def early(tick, carry):
        step(tick)

        @pl.when(tick == OWN_TICK)
        def _():
            own_block().start()

        return carry

    def part_here(part):
        for k in range(2):
            other = (1 - core) * 2 + k

            @pl.when(other < BLOCKS[part])
            def _(k=k, other=other):
                fac_copy(fac, part, other, fac_share.at[part, k], sibling).wait_recv()

        fac_split[part, 0], fac_split[part, 1] = split(fac[part])

    def first_columns(j, carry):
        step(FIRST_WORK + j)
        tile = pl.ds(pl.multiple_of(j * NB, NB), NB)
        high, low_part = split(three(fac_split[0, 0], fac_split[0, 1], *split(slab[0, :, tile])))
        c_high[0:NB, tile] = high
        c_low[0:NB, tile] = low_part
        left[:, tile] = slab[1, :, tile] - three(fac_split[1, 0], fac_split[1, 1], high, low_part)
        return carry

    def first_rows(i, carry):
        step(ROWS_WORK + i)
        block = pl.ds(pl.multiple_of(i * NB, NB), NB)
        first = three_t(*split(rows[0, block, :]), fac_split[0, 0], fac_split[0, 1])
        high, low_part = split(first)
        r_high[block, 0:NB] = high
        r_low[block, 0:NB] = low_part
        rest[block, :] = rows[1, block, :] - three_t(high, low_part, fac_split[1, 0], fac_split[1, 1])
        return carry

    @pl.when(jnp.logical_not(is_root))
    def _():
        lax.fori_loop(0, FIRST_WORK, early, 0)

    @pl.when(is_root)
    def _():
        own_block().start()

        def chunk_here(i, carry):
            row_copy(None, 1, 0, i * CHUNK, CHUNK).wait_recv()
            return carry

        first_ticks = FIRST_WORK - LAG * DEEPEST
        lax.fori_loop(0, first_ticks - sum(place < first_ticks for place in PLACES), chunk_here, 0)
        fac_copy(fac, 1, 3, fac_share.at[1, 1], sibling).wait_recv()
        each_fac(1, 1, begin)

        for s in range(2):
            @pl.when(prow != s)
            def _(s=s):
                def strip_here(j, carry):
                    slab_copy(None, s, 0, j * STRIP, STRIP).wait_recv()
                    return carry

                lax.fori_loop(0, STRIPS, strip_here, 0)

    part_here(0)
    part_here(1)
    lax.fori_loop(0, COLUMN_BLOCKS, first_columns, 0)
    lax.fori_loop(FIRST_WORK + COLUMN_BLOCKS, ROWS_WORK, early, 0)
    lax.fori_loop(0, ROW_BLOCKS, first_rows, 0)
    part_here(2)

    for j in range(COLUMN_BLOCKS):
        tile = pl.ds(j * NB, NB)
        high, low_part = split(three(fac_split[2, 0], fac_split[2, 1], *split(left[:, tile])))
        c_high[NB:2 * NB, tile] = high
        c_low[NB:2 * NB, tile] = low_part

    for i in range(2):
        block = pl.ds(i * ROWS // 2, ROWS // 2)
        high, low_part = split(three_t(*split(rest[block, :]), fac_split[2, 0], fac_split[2, 1]))
        r_high[block, NB:2 * NB] = high
        r_low[block, NB:2 * NB] = low_part

    own_block().wait()

    for k in range(2):
        for d in range(4):
            @pl.when(gives[k][d])
            def _(k=k, d=d):
                row_copy(None, k, d, 0, ROWS).wait_send()

    for s in range(2):
        for slot, condition in enumerate((along[s], across[s])):
            @pl.when(condition)
            def _(s=s, slot=slot):
                slab_copy(None, s, slot, 0, NB).wait_send()

    for part in range(3):
        for k in range(2):
            @pl.when(core * 2 + k < BLOCKS[part])
            def _(part=part, k=k):
                each_fac(part, k, finish)

        @pl.when(is_root)
        def _(part=part):
            root_fac(part, finish)

    for n, e, to_z in leads():
        @pl.when(gives_lead[n])
        def _(n=n, e=e, to_z=to_z):
            lead_copy(n, e, to_z).wait_send()


def make_panels(matrix):
    dma = pltpu.SemaphoreType.DMA
    vmem = pl.BlockSpec(memory_space=pltpu.VMEM)
    return pl.pallas_call(
        panels_kernel,
        out_shape=(
            jax.ShapeDtypeStruct((ROWS, COLS), F32),
            jax.ShapeDtypeStruct((ROWS, 2 * NB), BF16),
            jax.ShapeDtypeStruct((ROWS, 2 * NB), BF16),
            jax.ShapeDtypeStruct((2 * NB, COLS), BF16),
            jax.ShapeDtypeStruct((2 * NB, COLS), BF16),
        ),
        in_specs=[pl.BlockSpec(memory_space=pl.ANY)],
        out_specs=(vmem, vmem, vmem, vmem, vmem),
        scratch_shapes=[
            pltpu.VMEM((2, ROWS, NB), F32),
            pltpu.VMEM((2, NB, COLS), F32),
            pltpu.VMEM((3, NB, NB), F32),
            pltpu.VMEM((3, 2, NB, NB), BF16),
            pltpu.VMEM((ROWS, NB), F32),
            pltpu.VMEM((NB, COLS), F32),
            pltpu.VMEM((3, NB, NB), F32),
            pltpu.VMEM((3, NB, NB), F32),
            pltpu.VMEM((HALF, NB), F32),
            pltpu.VMEM((HALF, HALF), F32),
            pltpu.VMEM((2, HALF, HALF), F32),
            pltpu.VMEM((HALF, HALF), F32),
            dma((6,)),
            dma((2, 4)),
            dma((2, CHUNKS)),
            dma((2, 2)),
            dma((2, STRIPS)),
            dma((3, 2, 4)),
            dma((3, 2)),
            dma((3, 4)),
            dma((sum(BLOCKS),)),
            dma((3, 3, 4)),
            dma((3, 3)),
        ],
        compiler_params=pltpu.CompilerParams(
            collective_id=0, has_side_effects=True, vmem_limit_bytes=32 * 2**20
        ),
        cost_estimate=pl.CostEstimate(flops=2**30, bytes_accessed=2**24, transcendentals=0),
        name="panels",
    )(matrix)


def update_kernel(w_ref, r_high, r_low, c_high, c_low, out_ref):
    i = pl.program_id(0)
    prow, pcol = lax.axis_index("prow"), lax.axis_index("pcol")
    row_block = i * 8 + prow
    block = pl.ds(pl.multiple_of(i * NB, NB), NB)
    out_ref[...] = w_ref[block, :] - three(r_high[block, :], r_low[block, :], c_high[...], c_low[...])

    @pl.when(row_block < 2)
    def _():
        out_ref[...] = jnp.zeros((NB, COLS), F32)

    down = lax.broadcasted_iota(jnp.int32, (NB, NB), 0)
    right = lax.broadcasted_iota(jnp.int32, (NB, NB), 1)
    for k in range(2):
        @pl.when(jnp.logical_and(pcol == k, row_block >= k))
        def _(k=k):
            panel = pl.ds(k * NB, NB)
            value = r_high[block, panel].astype(F32) + r_low[block, panel].astype(F32)
            keep = jnp.logical_or(row_block > k, right <= down)
            out_ref[:, 0:NB] = jnp.where(keep, value, 0.0)


def update(matrix, *panels):
    vmem = pl.BlockSpec(memory_space=pltpu.VMEM)
    return pl.pallas_call(
        update_kernel,
        out_shape=jax.ShapeDtypeStruct((ROWS, COLS), F32),
        grid=(ROWS // NB,),
        in_specs=[vmem] * 5,
        out_specs=pl.BlockSpec((NB, COLS), lambda i: (i, 0)),
        compiler_params=pltpu.CompilerParams(vmem_limit_bytes=32 * 2**20),
        cost_estimate=pl.CostEstimate(
            flops=2 * 3 * ROWS * COLS * 2 * NB, bytes_accessed=2**24, transcendentals=0
        ),
        name="update",
    )(matrix, *panels)


def body(matrix):
    return update(*make_panels(matrix))


def solution(mesh):
    spec = P("prow", "pcol")
    return jax.shard_map(body, mesh=mesh, in_specs=(spec,), out_specs=spec, check_vma=False)
```

```python
import jax
import jax.numpy as jnp
from jax import lax
from jax.experimental import pallas as pl
from jax.experimental.pallas import tpu as pltpu

P = jax.sharding.PartitionSpec
MESH = pl.DeviceIdType.MESH
HI = lax.Precision.HIGHEST
F32 = jnp.float32
BF16 = jnp.bfloat16
NB = 256
HALF = NB // 2
ROWS = 2560
COLS = 1280
CHUNK = 64
CHUNKS = ROWS // CHUNK
STRIP = 16
STRIPS = NB // STRIP
BLOCKS = (3, 4, 3)
FIRST_MESSAGE = (0, 3, 7)
PLACES = (25, 27, 40)
ITEMS = CHUNKS + len(PLACES)
LAG = 4
DEEPEST = 5
TICKS = ITEMS + LAG * DEEPEST
SLAB_TICK = 12
OWN_TICK = 44
FIRST_WORK = PLACES[1] + LAG * DEEPEST + 1
ROWS_WORK = TICKS - ROWS // NB
COLUMN_BLOCKS = COLS // NB
ROW_BLOCKS = ROWS // NB
assert SLAB_TICK + LAG * DEEPEST + STRIPS <= FIRST_WORK == ROWS_WORK - COLUMN_BLOCKS
AHEAD = 6
PUMP = 5


def mm(a, b):
    return lax.dot_general(a, b, (((1,), (0,)), ((), ())), precision=HI, preferred_element_type=F32)


def mmt(a, b):
    return lax.dot_general(a, b, (((1,), (1,)), ((), ())), precision=HI, preferred_element_type=F32)


def split(v):
    high = v.astype(BF16)
    return high, (v - high.astype(F32)).astype(BF16)


def three(a_high, a_low, b_high, b_low, contract=0):
    def dot(p, q):
        return lax.dot_general(p, q, (((1,), (contract,)), ((), ())), preferred_element_type=F32)

    return dot(a_high, b_high) + dot(a_high, b_low) + dot(a_low, b_high)


def three_t(a_high, a_low, b_high, b_low):
    return three(a_high, a_low, b_high, b_low, 1)


def full(v):
    return jnp.broadcast_to(v, (8, 128))

def leaf(w, start):
    lane = lax.broadcasted_iota(jnp.int32, (8, 128), 1)
    sub = lax.broadcasted_iota(jnp.int32, (8, 128), 0)
    other = (lane < 64) if start else (lane >= 64)
    rows = [w[8 * i:8 * i + 8, :] for i in range(8)]
    out = []
    for b in range(8):
        c = start + 8 * b
        bc = {i: [full(rows[i][:, c + k:c + k + 1]) for k in range(8)] for i in range(b, 8)}
        e = {(l, k): full(bc[b][k][l:l + 1, :]) for k in range(8) for l in range(k, 8)}
        u = [full(rows[b][k:k + 1, :]) for k in range(8)]
        done = jnp.zeros((8, 128), F32)
        for k in range(8):
            inv = 1.0 / e[k, k]
            for m in range(k + 1, 8):
                t = e[m, k] * inv
                for l in range(m, 8):
                    e[l, m] = e[l, m] - t * e[l, k]
                u[m] = u[m] - t * u[k]
                for i in range(b + 1, 8):
                    bc[i][m] = bc[i][m] - t * bc[i][k]
            scaled = u[k] * inv
            for i in range(b + 1, 8):
                rows[i] = rows[i] - bc[i][k] * scaled
            done = jnp.where(sub == k, u[k] * lax.rsqrt(e[k, k]), done)
        out.append(jnp.where(other, done, 0.0))
    return jnp.concatenate(out, axis=0)


def chol128(s, pump):
    r = lax.broadcasted_iota(jnp.int32, (64, 128), 0)
    c = lax.broadcasted_iota(jnp.int32, (64, 128), 1)
    low = jnp.where(c == r, 1.0, 0.0)
    high = jnp.where(c == r + 64, 1.0, 0.0)
    first = leaf(jnp.where(c < 64, s[:64], high), 0)
    pump(0)
    ma = pltpu.roll(first, 64, 1)
    l21 = mmt(jnp.where(c < 64, s[64:], 0.0), ma)
    s22 = mmt(l21, l21)
    z = jnp.zeros((64, 64), F32)
    s22 = jnp.concatenate([z, s22], axis=1)
    t = mm(l21, ma)
    second = leaf(jnp.where(c < 64, low, s[64:] - s22), 64)
    pump(1)
    low_part = mm(second[:, :64], high - t)
    return jnp.concatenate([ma, low_part], axis=0)


PARENTS = (
    (
        (-1, 0, 3, 0, 8, 9, 10, 11, 12, 8, 14, 8, 0, 12, 15, 12),
        (1, -1, 14, 15, 5, 1, 5, 6, 9, 13, 9, 15, 13, 1, 13, 14),
    ),
    (
        (-1, 5, 6, 7, 0, 4, 7, 4, 4, 5, 11, 7, 8, 9, 10, 11),
        (3, -1, 1, 2, 7, 6, 2, 3, 11, 10, 6, 10, 15, 14, 2, 3),
    ),
)


def neighbour(chip, direction):
    y, x = chip // 4, chip % 4
    if direction < 2:
        return y * 4 + (x + (1, 3)[direction]) % 4
    return (y + (1, 3)[direction - 2]) % 4 * 4 + x


def depth(core, panel, chip):
    parent = PARENTS[core][panel][chip]
    return 0 if parent < 0 else 1 + depth(core, panel, parent)


def handled_at(core, panel, chip):
    return depth(core, panel, chip) if chip in PARENTS[core][panel] else DEEPEST


def senders(core, panel, direction):
    parents = PARENTS[core][panel]
    return [n for n in range(16) if parents[neighbour(n, direction)] == n]


(ROOT_GIVES,) = [d for d in range(4) if 0 in senders(1, 0, d)]


def panels_kernel(
    a_ref, w_ref, r_high, r_low, c_high, c_low, rows, slab, fac, fac_split, rest, left, leading, made, stage, lead, inv, low,
    local_sem, row_send, row_recv, slab_send, slab_recv,
    fac_send, fac_share, fac_give, fac_recv, lead_send, lead_recv,
):
    prow, pcol = lax.axis_index("prow"), lax.axis_index("pcol")
    z, core = prow // 2, prow % 2
    y, x = pcol // 4, pcol % 4
    both = jnp.logical_and
    is_root = both(core == 1, pcol == 0)
    gives_lead = (both(prow == 0, pcol == 0), both(prow == 1, pcol == 0), both(prow == 1, pcol == 1))

    def device(pz, pc, py, px):
        return {"prow": pz * 2 + pc, "pcol": py * 4 + px}

    def on_line(axis, step):
        if axis == "x":
            return device(z, core, y, (x + step) % 4)
        if axis == "y":
            return device(z, core, (y + step) % 4, x)
        return device((z + step) % 4, core, y, x)

    sibling = device(z, 1 - core, y, x)
    root = {"prow": z * 2 + 1, "pcol": 0}

    def own_block():
        return pltpu.make_async_copy(a_ref, w_ref, local_sem.at[5])

    barrier = pltpu.get_barrier_semaphore()

    def greet(target):
        pl.semaphore_signal(barrier, 1, device_id=target, device_id_type=MESH)

    for axis, steps in (("x", (1, 3)), ("y", (1, 3)), ("z", (1, 2, 3))):
        for step in steps:
            greet(on_line(axis, step))
    greet(sibling)

    @pl.when(both(is_root, z > 0))
    def _():
        greet({"prow": 0, "pcol": 0})
        greet({"prow": 1, "pcol": 1})

    @pl.when(both(core == 0, pcol == 1))
    def _():
        greet(root)

    extra = jnp.where(is_root, 1, 0) + jnp.where(jnp.logical_or(gives_lead[0], gives_lead[2]), 3, 0)
    index = core * 16 + pcol
    gives = [[None] * 4 for _ in range(2)]
    for k in range(2):
        for d in range(4):
            flag = jnp.int32(0)
            for c in range(2):
                for n in senders(c, k, d):
                    flag = flag + jnp.where(index == c * 16 + n, 1, 0)
            gives[k][d] = flag == 1
    depths = []
    for k in range(2):
        value = jnp.int32(0)
        for c in range(2):
            for n in range(16):
                value = value + jnp.where(index == c * 16 + n, handled_at(c, k, n), 0)
        depths.append(value)
    pl.semaphore_wait(barrier, 8 + extra)
    targets = (on_line("x", 1), on_line("x", 3), on_line("y", 1), on_line("y", 3))

    def row_copy(src, k, d, first, count):
        piece = pl.ds(first, count)
        return pltpu.make_async_remote_copy(
            src_ref=src.at[piece, pl.ds(0, NB)] if src is a_ref else rows.at[k, piece, :],
            dst_ref=rows.at[k, piece, :],
            send_sem=row_send.at[k, d],
            recv_sem=row_recv.at[k, first // CHUNK if count == CHUNK else 0],
            device_id=targets[d],
            device_id_type=MESH,
        )

    on_ring = (core == 0, core == jnp.where(pcol == 0, 0, 1))
    along = (both(on_ring[0], z < 3), both(on_ring[1], z != 1))
    start_of_one = both(pcol == 0, z == 0)
    across = (on_ring[0], jnp.logical_or(both(start_of_one, core == 1), both(on_ring[1], jnp.logical_not(start_of_one))))
    slab_depths = (
        z + jnp.where(on_ring[0], 0, 1),
        (4 - z) % 4 + jnp.where(on_ring[1], 0, 1) + jnp.where(pcol == 0, 1, 0),
    )

    def slab_copy(src, s, slot, first, count):
        piece = pl.ds(first, count)
        step = 1 if s == 0 else 3
        return pltpu.make_async_remote_copy(
            src_ref=a_ref.at[piece, :] if src is a_ref else slab.at[s, piece, :],
            dst_ref=slab.at[s, piece, :],
            send_sem=slab_send.at[s, slot],
            recv_sem=slab_recv.at[s, first // STRIP if count == STRIP else 0],
            device_id=on_line("z", step) if slot == 0 else sibling,
            device_id_type=MESH,
        )

    def own_rows(k):
        return pltpu.make_async_copy(a_ref.at[:, pl.ds(0, NB)], rows.at[k], local_sem.at[k])

    def own_slab(s):
        return pltpu.make_async_copy(a_ref.at[pl.ds(0, NB), :], slab.at[s], local_sem.at[2 + s])

    def own_lead():
        return pltpu.make_async_copy(a_ref.at[pl.ds(0, NB), pl.ds(0, NB)], leading.at[1], local_sem.at[4])

    def lead_copy(n, e, to_z):
        down, right, size = (0, 0, NB) if n == 1 else ((e + 1) // 2 * HALF, e // 2 * HALF, HALF)
        return pltpu.make_async_remote_copy(
            src_ref=a_ref.at[pl.ds(down, size), pl.ds(right, size)],
            dst_ref=leading.at[n, pl.ds(down, size), pl.ds(right, size)],
            send_sem=lead_send.at[n, e, to_z],
            recv_sem=lead_recv.at[n, e],
            device_id={"prow": 2 * to_z + 1, "pcol": 0},
            device_id_type=MESH,
        )

    def leads():
        for n in range(3):
            for e in range(1 if n == 1 else 3):
                for to_z in ((1, 3, 2) if n == 1 else (0, 1, 3, 2)):
                    yield n, e, to_z

    for n, e, to_z in leads():
        @pl.when(gives_lead[n])
        def _(n=n, e=e, to_z=to_z):
            lead_copy(n, e, to_z).start()

    @pl.when(gives_lead[1])
    def _():
        own_lead().start()

    for s in range(2):
        @pl.when(prow == s)
        def _(s=s):
            own_slab(s).start()

    for k in range(2):
        @pl.when(pcol == k)
        def _(k=k):
            own_rows(k).start()

    def send_chunk(src, k, i):
        for d in range(4):
            @pl.when(gives[k][d])
            def _(d=d):
                row_copy(src, k, d, i * CHUNK, CHUNK).start()

    def send_strip(src, s, j):
        @pl.when(along[s])
        def _():
            slab_copy(src, s, 0, j * STRIP, STRIP).start()

        @pl.when(across[s])
        def _():
            slab_copy(src, s, 1, j * STRIP, STRIP).start()

    def fac_block(ref, part, e):
        i, j = (e // 2, e % 2) if part == 1 else ((e + 1) // 2, e // 2)
        if not isinstance(e, int):
            i, j = pl.multiple_of(i * HALF, HALF), pl.multiple_of(j * HALF, HALF)
        else:
            i, j = i * HALF, j * HALF
        return ref.at[part, pl.ds(i, HALF), pl.ds(j, HALF)]

    def fac_copy(src, part, e, send_sem, target):
        return pltpu.make_async_remote_copy(
            src_ref=fac_block(src, part, e),
            dst_ref=fac_block(fac, part, e),
            send_sem=send_sem,
            recv_sem=fac_recv.at[FIRST_MESSAGE[part] + e],
            device_id=target,
            device_id_type=MESH,
        )

    def each_fac(part, k, act):
        e = core * 2 + k
        for d in range(4):
            @pl.when(gives[k][d])
            def _(d=d):
                act(fac_copy(fac, part, e, fac_send.at[part, k, d], targets[d]))
        act(fac_copy(fac, part, e, fac_share.at[part, k], sibling))

    def root_fac(part, act):
        for e, target in ((0, sibling), (1, {"prow": z * 2, "pcol": 1}), (3, {"prow": z * 2 + 1, "pcol": 1})):
            if e < BLOCKS[part]:
                act(fac_copy(made, part, e, fac_give.at[part, e], target))

    def begin(copy):
        copy.start()

    def finish(copy):
        copy.wait_send()

    def give_part(part):
        root_fac(part, begin)
        i, j = (1, 0) if part == 1 else (1, 1)
        span = (part, pl.ds(i * HALF, HALF), pl.ds(j * HALF, HALF))
        fac[span] = made[span]
        each_fac(part, 0, begin)

    def pass_rows(tick, parts):
        for k in range(2):
            n = tick - LAG * depths[k]
            skips = jnp.int32(0)
            special = n < 0
            for place in PLACES:
                skips = skips + jnp.where(n > place, 1, 0)
                special = jnp.logical_or(special, n == place)
            i = n - skips
            here = both(jnp.logical_not(special), n < ITEMS)
            mine = both(here, pcol == k)
            if k == 0:
                mine = both(mine, jnp.logical_not(is_root))

            @pl.when(both(here, pcol != k))
            def _(k=k, i=i):
                row_copy(None, k, 0, i * CHUNK, CHUNK).wait_recv()
                send_chunk(None, k, i)

            @pl.when(mine)
            def _(k=k, i=i):
                send_chunk(a_ref, k, i)

            for part in parts:
                now = both(n == PLACES[part], core * 2 + k < BLOCKS[part])
                if k == 0:
                    now = both(now, jnp.logical_not(is_root))

                @pl.when(now)
                def _(k=k, part=part):
                    fac_copy(fac, part, core * 2 + k, fac_share.at[part, k], sibling).wait_recv()
                    each_fac(part, k, begin)

    def pass_slab(tick):
        for s in range(2):
            j = tick - SLAB_TICK - LAG * slab_depths[s]
            here = both(j >= 0, j < STRIPS)

            @pl.when(both(here, prow != s))
            def _(s=s, j=j):
                slab_copy(None, s, 0, j * STRIP, STRIP).wait_recv()
                send_strip(None, s, j)

            @pl.when(both(both(tick < STRIPS, prow == s), jnp.logical_not(is_root)))
            def _(s=s):
                send_strip(a_ref, s, tick)

    for part in (0, 2):
        fac[part, 0:HALF, HALF:NB] = jnp.zeros((HALF, HALF), F32)

    @pl.when(is_root)
    def _():
        def pump(first, count):
            def one(i, carry):
                @pl.when(i < CHUNKS)
                def _():
                    row_copy(a_ref, 0, ROOT_GIVES, i * CHUNK, CHUNK).start()

                return carry

            lax.fori_loop(first, first + count, one, 0)

        pump(0, AHEAD)

        @pl.when(prow == 1)
        def _():
            def one(j, carry):
                send_strip(a_ref, 1, j)
                return carry

            lax.fori_loop(0, STRIPS, one, 0)

        lead_copy(0, 0, z).wait_recv()
        lead[...] = leading[0, 0:HALF, 0:HALF]

        def panel(k, carry):
            def half(h, inner):
                inv[h] = chol128(lead[...], lambda n: pump(AHEAD + (4 * k + 2 * h + n) * PUMP, PUMP))

                @pl.when(h == 0)
                def _():
                    @pl.when(k == 0)
                    def _():
                        for e in (1, 2):
                            lead_copy(0, e, z).wait_recv()
                        stage[...] = leading[0, HALF:NB, :]

                    @pl.when(k == 1)
                    def _():
                        for e in (1, 2):
                            lead_copy(2, e, z).wait_recv()
                        stage[...] = leading[2, HALF:NB, :] - mmt(made[1, HALF:NB, :], made[1])

                    low[...] = mmt(stage[:, 0:HALF], inv[0])
                    lead[...] = stage[:, HALF:NB] - mmt(low[...], low[...])

                return inner

            lax.fori_loop(0, 2, half, 0)
            made[2 * k, 0:HALF, 0:HALF] = inv[0]
            made[2 * k, 0:HALF, HALF:NB] = jnp.zeros((HALF, HALF), F32)
            made[2 * k, HALF:NB, HALF:NB] = inv[1]
            made[2 * k, HALF:NB, 0:HALF] = -mm(inv[1], mm(low[...], inv[0]))

            @pl.when(k == 0)
            def _():
                give_part(0)

                @pl.when(prow == 1)
                def _():
                    own_lead().wait()

                @pl.when(prow != 1)
                def _():
                    lead_copy(1, 0, z).wait_recv()

                made[1] = mmt(leading[1], made[0])
                lead_copy(2, 0, z).wait_recv()
                top = made[1, 0:HALF, :]
                lead[...] = leading[2, 0:HALF, 0:HALF] - mmt(top, top)
                give_part(1)

            @pl.when(k == 1)
            def _():
                give_part(2)

            return carry

        lax.fori_loop(0, 2, panel, 0)

    for k in range(2):
        @pl.when(pcol == k)
        def _(k=k):
            own_rows(k).wait()

    for s in range(2):
        @pl.when(prow == s)
        def _(s=s):
            own_slab(s).wait()

    def late(tick):
        pass_rows(tick, (2,))

    def early(tick, carry):
        pass_rows(tick, (0, 1, 2))
        pass_slab(tick)

        @pl.when(tick == OWN_TICK)
        def _():
            own_block().start()

        return carry

    def part_here(part):
        for k in range(2):
            other = (1 - core) * 2 + k

            @pl.when(other < BLOCKS[part])
            def _(k=k, other=other):
                fac_copy(fac, part, other, fac_share.at[part, k], sibling).wait_recv()

        fac_split[part, 0], fac_split[part, 1] = split(fac[part])

    def first_columns(j, carry):
        late(FIRST_WORK + j)
        tile = pl.ds(pl.multiple_of(j * NB, NB), NB)
        high, low_part = split(three(fac_split[0, 0], fac_split[0, 1], *split(slab[0, :, tile])))
        c_high[0:NB, tile] = high
        c_low[0:NB, tile] = low_part
        left[:, tile] = slab[1, :, tile] - three(fac_split[1, 0], fac_split[1, 1], high, low_part)
        return carry

    def first_rows(i, carry):
        late(ROWS_WORK + i)
        block = pl.ds(pl.multiple_of(i * NB, NB), NB)
        first = three_t(*split(rows[0, block, :]), fac_split[0, 0], fac_split[0, 1])
        high, low_part = split(first)
        r_high[block, 0:NB] = high
        r_low[block, 0:NB] = low_part
        rest[block, :] = rows[1, block, :] - three_t(high, low_part, fac_split[1, 0], fac_split[1, 1])
        return carry

    @pl.when(jnp.logical_not(is_root))
    def _():
        lax.fori_loop(0, FIRST_WORK, early, 0)

    @pl.when(is_root)
    def _():
        own_block().start()

        def chunk_here(i, carry):
            row_copy(None, 1, 0, i * CHUNK, CHUNK).wait_recv()
            return carry

        first_ticks = FIRST_WORK - LAG * DEEPEST
        lax.fori_loop(0, first_ticks - sum(place < first_ticks for place in PLACES), chunk_here, 0)
        fac_copy(fac, 1, 3, fac_share.at[1, 1], sibling).wait_recv()
        each_fac(1, 1, begin)

        for s in range(2):
            @pl.when(prow != s)
            def _(s=s):
                def strip_here(j, carry):
                    slab_copy(None, s, 0, j * STRIP, STRIP).wait_recv()
                    return carry

                lax.fori_loop(0, STRIPS, strip_here, 0)

    part_here(0)
    part_here(1)
    lax.fori_loop(0, COLUMN_BLOCKS, first_columns, 0)
    lax.fori_loop(0, ROW_BLOCKS, first_rows, 0)
    part_here(2)

    for j in range(COLUMN_BLOCKS):
        tile = pl.ds(j * NB, NB)
        high, low_part = split(three(fac_split[2, 0], fac_split[2, 1], *split(left[:, tile])))
        c_high[NB:2 * NB, tile] = high
        c_low[NB:2 * NB, tile] = low_part

    for i in range(2):
        block = pl.ds(i * ROWS // 2, ROWS // 2)
        high, low_part = split(three_t(*split(rest[block, :]), fac_split[2, 0], fac_split[2, 1]))
        r_high[block, NB:2 * NB] = high
        r_low[block, NB:2 * NB] = low_part

    own_block().wait()

    for k in range(2):
        for d in range(4):
            @pl.when(gives[k][d])
            def _(k=k, d=d):
                row_copy(None, k, d, 0, ROWS).wait_send()

    for s in range(2):
        for slot, condition in enumerate((along[s], across[s])):
            @pl.when(condition)
            def _(s=s, slot=slot):
                slab_copy(None, s, slot, 0, NB).wait_send()

    for part in range(3):
        for k in range(2):
            @pl.when(core * 2 + k < BLOCKS[part])
            def _(part=part, k=k):
                each_fac(part, k, finish)

        @pl.when(is_root)
        def _(part=part):
            root_fac(part, finish)

    for n, e, to_z in leads():
        @pl.when(gives_lead[n])
        def _(n=n, e=e, to_z=to_z):
            lead_copy(n, e, to_z).wait_send()


def make_panels(matrix):
    dma = pltpu.SemaphoreType.DMA
    vmem = pl.BlockSpec(memory_space=pltpu.VMEM)
    return pl.pallas_call(
        panels_kernel,
        out_shape=(
            jax.ShapeDtypeStruct((ROWS, COLS), F32),
            jax.ShapeDtypeStruct((ROWS, 2 * NB), BF16),
            jax.ShapeDtypeStruct((ROWS, 2 * NB), BF16),
            jax.ShapeDtypeStruct((2 * NB, COLS), BF16),
            jax.ShapeDtypeStruct((2 * NB, COLS), BF16),
        ),
        in_specs=[pl.BlockSpec(memory_space=pl.ANY)],
        out_specs=(vmem, vmem, vmem, vmem, vmem),
        scratch_shapes=[
            pltpu.VMEM((2, ROWS, NB), F32),
            pltpu.VMEM((2, NB, COLS), F32),
            pltpu.VMEM((3, NB, NB), F32),
            pltpu.VMEM((3, 2, NB, NB), BF16),
            pltpu.VMEM((ROWS, NB), F32),
            pltpu.VMEM((NB, COLS), F32),
            pltpu.VMEM((3, NB, NB), F32),
            pltpu.VMEM((3, NB, NB), F32),
            pltpu.VMEM((HALF, NB), F32),
            pltpu.VMEM((HALF, HALF), F32),
            pltpu.VMEM((2, HALF, HALF), F32),
            pltpu.VMEM((HALF, HALF), F32),
            dma((6,)),
            dma((2, 4)),
            dma((2, CHUNKS)),
            dma((2, 2)),
            dma((2, STRIPS)),
            dma((3, 2, 4)),
            dma((3, 2)),
            dma((3, 4)),
            dma((sum(BLOCKS),)),
            dma((3, 3, 4)),
            dma((3, 3)),
        ],
        compiler_params=pltpu.CompilerParams(
            collective_id=0, has_side_effects=True, vmem_limit_bytes=32 * 2**20
        ),
        cost_estimate=pl.CostEstimate(flops=2**30, bytes_accessed=2**24, transcendentals=0),
        name="panels",
    )(matrix)


def update_kernel(w_ref, r_high, r_low, c_high, c_low, out_ref):
    i = pl.program_id(0)
    prow, pcol = lax.axis_index("prow"), lax.axis_index("pcol")
    row_block = i * 8 + prow
    block = pl.ds(pl.multiple_of(i * NB, NB), NB)
    out_ref[...] = w_ref[block, :] - three(r_high[block, :], r_low[block, :], c_high[...], c_low[...])

    @pl.when(row_block < 2)
    def _():
        out_ref[...] = jnp.zeros((NB, COLS), F32)

    down = lax.broadcasted_iota(jnp.int32, (NB, NB), 0)
    right = lax.broadcasted_iota(jnp.int32, (NB, NB), 1)
    for k in range(2):
        @pl.when(jnp.logical_and(pcol == k, row_block >= k))
        def _(k=k):
            panel = pl.ds(k * NB, NB)
            value = r_high[block, panel].astype(F32) + r_low[block, panel].astype(F32)
            keep = jnp.logical_or(row_block > k, right <= down)
            out_ref[:, 0:NB] = jnp.where(keep, value, 0.0)


def update(matrix, *panels):
    vmem = pl.BlockSpec(memory_space=pltpu.VMEM)
    return pl.pallas_call(
        update_kernel,
        out_shape=jax.ShapeDtypeStruct((ROWS, COLS), F32),
        grid=(ROWS // NB,),
        in_specs=[vmem] * 5,
        out_specs=pl.BlockSpec((NB, COLS), lambda i: (i, 0)),
        compiler_params=pltpu.CompilerParams(vmem_limit_bytes=32 * 2**20),
        cost_estimate=pl.CostEstimate(
            flops=2 * 3 * ROWS * COLS * 2 * NB, bytes_accessed=2**24, transcendentals=0
        ),
        name="update",
    )(matrix, *panels)


def body(matrix):
    return update(*make_panels(matrix))


def solution(mesh):
    spec = P("prow", "pcol")
    return jax.shard_map(body, mesh=mesh, in_specs=(spec,), out_specs=spec, check_vma=False)
```

```python
import jax
import jax.numpy as jnp
from jax import lax
from jax.experimental import pallas as pl
from jax.experimental.pallas import tpu as pltpu

P = jax.sharding.PartitionSpec
MESH = pl.DeviceIdType.MESH
HI = lax.Precision.HIGHEST
F32 = jnp.float32
BF16 = jnp.bfloat16
NB = 256
HALF = NB // 2
ROWS = 2560
COLS = 1280
CHUNK = 64
CHUNKS = ROWS // CHUNK
STRIP = 16
STRIPS = NB // STRIP
BLOCKS = (3, 4, 3)
FIRST_MESSAGE = (0, 3, 7)
PLACES = (25, 27, 40)
ITEMS = CHUNKS + len(PLACES)
LAG = 4
DEEPEST = 5
TICKS = ITEMS + LAG * DEEPEST
SLAB_TICK = 7
SLAB_TICKS = STRIPS * 4 // 3
OWN_TICK = 44
FIRST_WORK = PLACES[1] + LAG * DEEPEST + 1
ROWS_WORK = TICKS - ROWS // NB
COLUMN_BLOCKS = COLS // NB
ROW_BLOCKS = ROWS // NB
assert SLAB_TICK + LAG * DEEPEST + SLAB_TICKS <= FIRST_WORK == ROWS_WORK - COLUMN_BLOCKS
AHEAD = 6
PUMP = 5


def mm(a, b):
    return lax.dot_general(a, b, (((1,), (0,)), ((), ())), precision=HI, preferred_element_type=F32)


def mmt(a, b):
    return lax.dot_general(a, b, (((1,), (1,)), ((), ())), precision=HI, preferred_element_type=F32)


def split(v):
    high = v.astype(BF16)
    return high, (v - high.astype(F32)).astype(BF16)


def three(a_high, a_low, b_high, b_low, contract=0):
    def dot(p, q):
        return lax.dot_general(p, q, (((1,), (contract,)), ((), ())), preferred_element_type=F32)

    return dot(a_high, b_high) + dot(a_high, b_low) + dot(a_low, b_high)


def three_t(a_high, a_low, b_high, b_low):
    return three(a_high, a_low, b_high, b_low, 1)


def full(v):
    return jnp.broadcast_to(v, (8, 128))

def leaf(w, start):
    lane = lax.broadcasted_iota(jnp.int32, (8, 128), 1)
    sub = lax.broadcasted_iota(jnp.int32, (8, 128), 0)
    other = (lane < 64) if start else (lane >= 64)
    rows = [w[8 * i:8 * i + 8, :] for i in range(8)]
    out = []
    for b in range(8):
        c = start + 8 * b
        bc = {i: [full(rows[i][:, c + k:c + k + 1]) for k in range(8)] for i in range(b, 8)}
        e = {(l, k): full(bc[b][k][l:l + 1, :]) for k in range(8) for l in range(k, 8)}
        u = [full(rows[b][k:k + 1, :]) for k in range(8)]
        done = jnp.zeros((8, 128), F32)
        for k in range(8):
            inv = 1.0 / e[k, k]
            for m in range(k + 1, 8):
                t = e[m, k] * inv
                for l in range(m, 8):
                    e[l, m] = e[l, m] - t * e[l, k]
                u[m] = u[m] - t * u[k]
                for i in range(b + 1, 8):
                    bc[i][m] = bc[i][m] - t * bc[i][k]
            scaled = u[k] * inv
            for i in range(b + 1, 8):
                rows[i] = rows[i] - bc[i][k] * scaled
            done = jnp.where(sub == k, u[k] * lax.rsqrt(e[k, k]), done)
        out.append(jnp.where(other, done, 0.0))
    return jnp.concatenate(out, axis=0)


def chol128(s, pump):
    r = lax.broadcasted_iota(jnp.int32, (64, 128), 0)
    c = lax.broadcasted_iota(jnp.int32, (64, 128), 1)
    low = jnp.where(c == r, 1.0, 0.0)
    high = jnp.where(c == r + 64, 1.0, 0.0)
    first = leaf(jnp.where(c < 64, s[:64], high), 0)
    pump(0)
    ma = pltpu.roll(first, 64, 1)
    l21 = mmt(jnp.where(c < 64, s[64:], 0.0), ma)
    s22 = mmt(l21, l21)
    z = jnp.zeros((64, 64), F32)
    s22 = jnp.concatenate([z, s22], axis=1)
    t = mm(l21, ma)
    second = leaf(jnp.where(c < 64, low, s[64:] - s22), 64)
    pump(1)
    low_part = mm(second[:, :64], high - t)
    return jnp.concatenate([ma, low_part], axis=0)


PARENTS = (
    (
        (-1, 0, 3, 0, 8, 9, 10, 11, 12, 8, 14, 8, 0, 12, 15, 12),
        (1, -1, 14, 15, 5, 1, 5, 6, 9, 13, 9, 15, 13, 1, 13, 14),
    ),
    (
        (-1, 5, 6, 7, 0, 4, 7, 4, 4, 5, 11, 7, 8, 9, 10, 11),
        (3, -1, 1, 2, 7, 6, 2, 3, 11, 10, 6, 10, 15, 14, 2, 3),
    ),
)


def neighbour(chip, direction):
    y, x = chip // 4, chip % 4
    if direction < 2:
        return y * 4 + (x + (1, 3)[direction]) % 4
    return (y + (1, 3)[direction - 2]) % 4 * 4 + x


def depth(core, panel, chip):
    parent = PARENTS[core][panel][chip]
    return 0 if parent < 0 else 1 + depth(core, panel, parent)


def handled_at(core, panel, chip):
    return depth(core, panel, chip) if chip in PARENTS[core][panel] else DEEPEST


def senders(core, panel, direction):
    parents = PARENTS[core][panel]
    return [n for n in range(16) if parents[neighbour(n, direction)] == n]


(ROOT_GIVES,) = [d for d in range(4) if 0 in senders(1, 0, d)]


def panels_kernel(
    a_ref, w_ref, r_high, r_low, c_high, c_low, rows, slab, fac, fac_split, rest, left, leading, made, stage, lead, inv, low,
    local_sem, row_send, row_recv, slab_send, slab_recv,
    fac_send, fac_share, fac_give, fac_recv, lead_send, lead_recv,
):
    prow, pcol = lax.axis_index("prow"), lax.axis_index("pcol")
    z, core = prow // 2, prow % 2
    y, x = pcol // 4, pcol % 4
    both = jnp.logical_and
    is_root = both(core == 1, pcol == 0)
    gives_lead = (both(prow == 0, pcol == 0), both(prow == 1, pcol == 0), both(prow == 1, pcol == 1))

    def device(pz, pc, py, px):
        return {"prow": pz * 2 + pc, "pcol": py * 4 + px}

    def on_line(axis, step):
        if axis == "x":
            return device(z, core, y, (x + step) % 4)
        if axis == "y":
            return device(z, core, (y + step) % 4, x)
        return device((z + step) % 4, core, y, x)

    sibling = device(z, 1 - core, y, x)
    root = {"prow": z * 2 + 1, "pcol": 0}

    def own_block():
        return pltpu.make_async_copy(a_ref, w_ref, local_sem.at[5])

    barrier = pltpu.get_barrier_semaphore()

    def greet(target):
        pl.semaphore_signal(barrier, 1, device_id=target, device_id_type=MESH)

    for axis, steps in (("x", (1, 3)), ("y", (1, 3)), ("z", (1, 2, 3))):
        for step in steps:
            greet(on_line(axis, step))
    greet(sibling)

    @pl.when(both(is_root, z > 0))
    def _():
        greet({"prow": 0, "pcol": 0})
        greet({"prow": 1, "pcol": 1})

    @pl.when(both(core == 0, pcol == 1))
    def _():
        greet(root)

    extra = jnp.where(is_root, 1, 0) + jnp.where(jnp.logical_or(gives_lead[0], gives_lead[2]), 3, 0)
    index = core * 16 + pcol
    gives = [[None] * 4 for _ in range(2)]
    for k in range(2):
        for d in range(4):
            flag = jnp.int32(0)
            for c in range(2):
                for n in senders(c, k, d):
                    flag = flag + jnp.where(index == c * 16 + n, 1, 0)
            gives[k][d] = flag == 1
    depths = []
    for k in range(2):
        value = jnp.int32(0)
        for c in range(2):
            for n in range(16):
                value = value + jnp.where(index == c * 16 + n, handled_at(c, k, n), 0)
        depths.append(value)
    pl.semaphore_wait(barrier, 8 + extra)
    targets = (on_line("x", 1), on_line("x", 3), on_line("y", 1), on_line("y", 3))

    def row_copy(src, k, d, first, count):
        piece = pl.ds(first, count)
        return pltpu.make_async_remote_copy(
            src_ref=src.at[piece, pl.ds(0, NB)] if src is a_ref else rows.at[k, piece, :],
            dst_ref=rows.at[k, piece, :],
            send_sem=row_send.at[k, d],
            recv_sem=row_recv.at[k, first // CHUNK if count == CHUNK else 0],
            device_id=targets[d],
            device_id_type=MESH,
        )

    on_ring = (core == 0, core == jnp.where(pcol == 0, 0, 1))
    along = (both(on_ring[0], z < 3), both(on_ring[1], z != 1))
    start_of_one = both(pcol == 0, z == 0)
    across = (on_ring[0], jnp.logical_or(both(start_of_one, core == 1), both(on_ring[1], jnp.logical_not(start_of_one))))
    slab_depths = (
        z + jnp.where(on_ring[0], 0, 1),
        (4 - z) % 4 + jnp.where(on_ring[1], 0, 1) + jnp.where(pcol == 0, 1, 0),
    )

    def slab_copy(src, s, slot, first, count):
        piece = pl.ds(first, count)
        step = 1 if s == 0 else 3
        return pltpu.make_async_remote_copy(
            src_ref=a_ref.at[piece, :] if src is a_ref else slab.at[s, piece, :],
            dst_ref=slab.at[s, piece, :],
            send_sem=slab_send.at[s, slot],
            recv_sem=slab_recv.at[s, first // STRIP if count == STRIP else 0],
            device_id=on_line("z", step) if slot == 0 else sibling,
            device_id_type=MESH,
        )

    def own_rows(k):
        return pltpu.make_async_copy(a_ref.at[:, pl.ds(0, NB)], rows.at[k], local_sem.at[k])

    def own_slab(s):
        return pltpu.make_async_copy(a_ref.at[pl.ds(0, NB), :], slab.at[s], local_sem.at[2 + s])

    def own_lead():
        return pltpu.make_async_copy(a_ref.at[pl.ds(0, NB), pl.ds(0, NB)], leading.at[1], local_sem.at[4])

    def lead_copy(n, e, to_z):
        down, right, size = (0, 0, NB) if n == 1 else ((e + 1) // 2 * HALF, e // 2 * HALF, HALF)
        return pltpu.make_async_remote_copy(
            src_ref=a_ref.at[pl.ds(down, size), pl.ds(right, size)],
            dst_ref=leading.at[n, pl.ds(down, size), pl.ds(right, size)],
            send_sem=lead_send.at[n, e, to_z],
            recv_sem=lead_recv.at[n, e],
            device_id={"prow": 2 * to_z + 1, "pcol": 0},
            device_id_type=MESH,
        )

    def leads():
        for n in range(3):
            for e in range(1 if n == 1 else 3):
                for to_z in ((1, 3, 2) if n == 1 else (0, 1, 3, 2)):
                    yield n, e, to_z

    for n, e, to_z in leads():
        @pl.when(gives_lead[n])
        def _(n=n, e=e, to_z=to_z):
            lead_copy(n, e, to_z).start()

    @pl.when(gives_lead[1])
    def _():
        own_lead().start()

    for s in range(2):
        @pl.when(prow == s)
        def _(s=s):
            own_slab(s).start()

    for k in range(2):
        @pl.when(pcol == k)
        def _(k=k):
            own_rows(k).start()

    def send_chunk(src, k, i):
        for d in range(4):
            @pl.when(gives[k][d])
            def _(d=d):
                row_copy(src, k, d, i * CHUNK, CHUNK).start()

    def send_strip(src, s, j):
        @pl.when(along[s])
        def _():
            slab_copy(src, s, 0, j * STRIP, STRIP).start()

        @pl.when(across[s])
        def _():
            slab_copy(src, s, 1, j * STRIP, STRIP).start()

    def fac_block(ref, part, e):
        i, j = (e // 2, e % 2) if part == 1 else ((e + 1) // 2, e // 2)
        if not isinstance(e, int):
            i, j = pl.multiple_of(i * HALF, HALF), pl.multiple_of(j * HALF, HALF)
        else:
            i, j = i * HALF, j * HALF
        return ref.at[part, pl.ds(i, HALF), pl.ds(j, HALF)]

    def fac_copy(src, part, e, send_sem, target):
        return pltpu.make_async_remote_copy(
            src_ref=fac_block(src, part, e),
            dst_ref=fac_block(fac, part, e),
            send_sem=send_sem,
            recv_sem=fac_recv.at[FIRST_MESSAGE[part] + e],
            device_id=target,
            device_id_type=MESH,
        )

    def each_fac(part, k, act):
        e = core * 2 + k
        for d in range(4):
            @pl.when(gives[k][d])
            def _(d=d):
                act(fac_copy(fac, part, e, fac_send.at[part, k, d], targets[d]))
        act(fac_copy(fac, part, e, fac_share.at[part, k], sibling))

    def root_fac(part, act):
        for e, target in ((0, sibling), (1, {"prow": z * 2, "pcol": 1}), (3, {"prow": z * 2 + 1, "pcol": 1})):
            if e < BLOCKS[part]:
                act(fac_copy(made, part, e, fac_give.at[part, e], target))

    def begin(copy):
        copy.start()

    def finish(copy):
        copy.wait_send()

    def give_part(part):
        root_fac(part, begin)
        i, j = (1, 0) if part == 1 else (1, 1)
        span = (part, pl.ds(i * HALF, HALF), pl.ds(j * HALF, HALF))
        fac[span] = made[span]
        each_fac(part, 0, begin)

    def pass_rows(tick, begin_tick, end_tick):
        parts = [
            part for part, place in enumerate(PLACES)
            if begin_tick - LAG * DEEPEST <= place < end_tick
        ]
        passed = sum(place < begin_tick - LAG * DEEPEST for place in PLACES)
        for k in range(2):
            n = tick - LAG * depths[k]
            skips = jnp.int32(passed)
            special = n < 0
            for part in parts:
                skips = skips + jnp.where(n > PLACES[part], 1, 0)
                special = jnp.logical_or(special, n == PLACES[part])
            i = n - skips
            here = both(jnp.logical_not(special), n < ITEMS)
            mine = both(here, pcol == k)
            if k == 0:
                mine = both(mine, jnp.logical_not(is_root))

            @pl.when(both(here, pcol != k))
            def _(k=k, i=i):
                row_copy(None, k, 0, i * CHUNK, CHUNK).wait_recv()
                send_chunk(None, k, i)

            @pl.when(mine)
            def _(k=k, i=i):
                send_chunk(a_ref, k, i)

            for part in parts:
                now = both(n == PLACES[part], core * 2 + k < BLOCKS[part])
                if k == 0:
                    now = both(now, jnp.logical_not(is_root))

                @pl.when(now)
                def _(k=k, part=part):
                    fac_copy(fac, part, core * 2 + k, fac_share.at[part, k], sibling).wait_recv()
                    each_fac(part, k, begin)

    def pass_slab(tick):
        for s in range(2):
            turn = (tick - SLAB_TICK - LAG * slab_depths[s]) * 3
            j = turn // 4
            here = both(both(turn >= 0, turn % 4 < 3), j < STRIPS)

            @pl.when(both(here, prow != s))
            def _(s=s, j=j):
                slab_copy(None, s, 0, j * STRIP, STRIP).wait_recv()
                send_strip(None, s, j)

    def source_slab(tick):
        for s in range(2):
            @pl.when(both(prow == s, jnp.logical_not(is_root)))
            def _(s=s):
                send_strip(a_ref, s, tick)

    for part in (0, 2):
        fac[part, 0:HALF, HALF:NB] = jnp.zeros((HALF, HALF), F32)

    @pl.when(is_root)
    def _():
        def pump(first, count):
            def one(i, carry):
                @pl.when(i < CHUNKS)
                def _():
                    row_copy(a_ref, 0, ROOT_GIVES, i * CHUNK, CHUNK).start()

                return carry

            lax.fori_loop(first, first + count, one, 0)

        pump(0, AHEAD)

        @pl.when(prow == 1)
        def _():
            def one(j, carry):
                send_strip(a_ref, 1, j)
                return carry

            lax.fori_loop(0, STRIPS, one, 0)

        lead_copy(0, 0, z).wait_recv()
        lead[...] = leading[0, 0:HALF, 0:HALF]

        def panel(k, carry):
            def half(h, inner):
                inv[h] = chol128(lead[...], lambda n: pump(AHEAD + (4 * k + 2 * h + n) * PUMP, PUMP))

                @pl.when(h == 0)
                def _():
                    @pl.when(k == 0)
                    def _():
                        for e in (1, 2):
                            lead_copy(0, e, z).wait_recv()
                        stage[...] = leading[0, HALF:NB, :]

                    @pl.when(k == 1)
                    def _():
                        for e in (1, 2):
                            lead_copy(2, e, z).wait_recv()
                        stage[...] = leading[2, HALF:NB, :] - mmt(made[1, HALF:NB, :], made[1])

                    low[...] = mmt(stage[:, 0:HALF], inv[0])
                    lead[...] = stage[:, HALF:NB] - mmt(low[...], low[...])

                return inner

            lax.fori_loop(0, 2, half, 0)
            made[2 * k, 0:HALF, 0:HALF] = inv[0]
            made[2 * k, 0:HALF, HALF:NB] = jnp.zeros((HALF, HALF), F32)
            made[2 * k, HALF:NB, HALF:NB] = inv[1]
            made[2 * k, HALF:NB, 0:HALF] = -mm(inv[1], mm(low[...], inv[0]))

            @pl.when(k == 0)
            def _():
                give_part(0)

                @pl.when(prow == 1)
                def _():
                    own_lead().wait()

                @pl.when(prow != 1)
                def _():
                    lead_copy(1, 0, z).wait_recv()

                made[1] = mmt(leading[1], made[0])
                lead_copy(2, 0, z).wait_recv()
                top = made[1, 0:HALF, :]
                lead[...] = leading[2, 0:HALF, 0:HALF] - mmt(top, top)
                give_part(1)

            @pl.when(k == 1)
            def _():
                give_part(2)

            return carry

        lax.fori_loop(0, 2, panel, 0)

    for k in range(2):
        @pl.when(pcol == k)
        def _(k=k):
            own_rows(k).wait()

    for s in range(2):
        @pl.when(prow == s)
        def _(s=s):
            own_slab(s).wait()

    def ticks(begin_tick, end_tick, sends, passes):
        def one(tick, carry):
            pass_rows(tick, begin_tick, end_tick)
            if passes:
                pass_slab(tick)
            if sends:
                source_slab(tick)
            return carry

        lax.fori_loop(begin_tick, end_tick, one, 0)

    def late(tick):
        pass_rows(tick, FIRST_WORK, TICKS)

    def part_here(part):
        for k in range(2):
            other = (1 - core) * 2 + k

            @pl.when(other < BLOCKS[part])
            def _(k=k, other=other):
                fac_copy(fac, part, other, fac_share.at[part, k], sibling).wait_recv()

        fac_split[part, 0], fac_split[part, 1] = split(fac[part])

    def first_columns(j, carry):
        late(FIRST_WORK + j)
        tile = pl.ds(pl.multiple_of(j * NB, NB), NB)
        high, low_part = split(three(fac_split[0, 0], fac_split[0, 1], *split(slab[0, :, tile])))
        c_high[0:NB, tile] = high
        c_low[0:NB, tile] = low_part
        left[:, tile] = slab[1, :, tile] - three(fac_split[1, 0], fac_split[1, 1], high, low_part)
        return carry

    def first_rows(i, carry):
        late(ROWS_WORK + i)
        block = pl.ds(pl.multiple_of(i * NB, NB), NB)
        first = three_t(*split(rows[0, block, :]), fac_split[0, 0], fac_split[0, 1])
        high, low_part = split(first)
        r_high[block, 0:NB] = high
        r_low[block, 0:NB] = low_part
        rest[block, :] = rows[1, block, :] - three_t(high, low_part, fac_split[1, 0], fac_split[1, 1])
        return carry

    @pl.when(jnp.logical_not(is_root))
    def _():
        ticks(0, SLAB_TICK + LAG, True, False)
        ticks(SLAB_TICK + LAG, STRIPS, True, True)
        ticks(STRIPS, PLACES[0], False, True)
        ticks(PLACES[0], OWN_TICK, False, True)
        own_block().start()
        ticks(OWN_TICK, FIRST_WORK, False, True)

    @pl.when(is_root)
    def _():
        own_block().start()

        def chunk_here(i, carry):
            row_copy(None, 1, 0, i * CHUNK, CHUNK).wait_recv()
            return carry

        first_ticks = FIRST_WORK - LAG * DEEPEST
        lax.fori_loop(0, first_ticks - sum(place < first_ticks for place in PLACES), chunk_here, 0)
        fac_copy(fac, 1, 3, fac_share.at[1, 1], sibling).wait_recv()
        each_fac(1, 1, begin)

        for s in range(2):
            @pl.when(prow != s)
            def _(s=s):
                def strip_here(j, carry):
                    slab_copy(None, s, 0, j * STRIP, STRIP).wait_recv()
                    return carry

                lax.fori_loop(0, STRIPS, strip_here, 0)

    part_here(0)
    part_here(1)
    lax.fori_loop(0, COLUMN_BLOCKS, first_columns, 0)
    lax.fori_loop(0, ROW_BLOCKS, first_rows, 0)
    part_here(2)

    for j in range(COLUMN_BLOCKS):
        tile = pl.ds(j * NB, NB)
        high, low_part = split(three(fac_split[2, 0], fac_split[2, 1], *split(left[:, tile])))
        c_high[NB:2 * NB, tile] = high
        c_low[NB:2 * NB, tile] = low_part

    for i in range(2):
        block = pl.ds(i * ROWS // 2, ROWS // 2)
        high, low_part = split(three_t(*split(rest[block, :]), fac_split[2, 0], fac_split[2, 1]))
        r_high[block, NB:2 * NB] = high
        r_low[block, NB:2 * NB] = low_part

    own_block().wait()

    for k in range(2):
        for d in range(4):
            @pl.when(gives[k][d])
            def _(k=k, d=d):
                row_copy(None, k, d, 0, ROWS).wait_send()

    for s in range(2):
        for slot, condition in enumerate((along[s], across[s])):
            @pl.when(condition)
            def _(s=s, slot=slot):
                slab_copy(None, s, slot, 0, NB).wait_send()

    for part in range(3):
        for k in range(2):
            @pl.when(core * 2 + k < BLOCKS[part])
            def _(part=part, k=k):
                each_fac(part, k, finish)

        @pl.when(is_root)
        def _(part=part):
            root_fac(part, finish)

    for n, e, to_z in leads():
        @pl.when(gives_lead[n])
        def _(n=n, e=e, to_z=to_z):
            lead_copy(n, e, to_z).wait_send()


def make_panels(matrix):
    dma = pltpu.SemaphoreType.DMA
    vmem = pl.BlockSpec(memory_space=pltpu.VMEM)
    return pl.pallas_call(
        panels_kernel,
        out_shape=(
            jax.ShapeDtypeStruct((ROWS, COLS), F32),
            jax.ShapeDtypeStruct((ROWS, 2 * NB), BF16),
            jax.ShapeDtypeStruct((ROWS, 2 * NB), BF16),
            jax.ShapeDtypeStruct((2 * NB, COLS), BF16),
            jax.ShapeDtypeStruct((2 * NB, COLS), BF16),
        ),
        in_specs=[pl.BlockSpec(memory_space=pl.ANY)],
        out_specs=(vmem, vmem, vmem, vmem, vmem),
        scratch_shapes=[
            pltpu.VMEM((2, ROWS, NB), F32),
            pltpu.VMEM((2, NB, COLS), F32),
            pltpu.VMEM((3, NB, NB), F32),
            pltpu.VMEM((3, 2, NB, NB), BF16),
            pltpu.VMEM((ROWS, NB), F32),
            pltpu.VMEM((NB, COLS), F32),
            pltpu.VMEM((3, NB, NB), F32),
            pltpu.VMEM((3, NB, NB), F32),
            pltpu.VMEM((HALF, NB), F32),
            pltpu.VMEM((HALF, HALF), F32),
            pltpu.VMEM((2, HALF, HALF), F32),
            pltpu.VMEM((HALF, HALF), F32),
            dma((6,)),
            dma((2, 4)),
            dma((2, CHUNKS)),
            dma((2, 2)),
            dma((2, STRIPS)),
            dma((3, 2, 4)),
            dma((3, 2)),
            dma((3, 4)),
            dma((sum(BLOCKS),)),
            dma((3, 3, 4)),
            dma((3, 3)),
        ],
        compiler_params=pltpu.CompilerParams(
            collective_id=0, has_side_effects=True, vmem_limit_bytes=32 * 2**20
        ),
        cost_estimate=pl.CostEstimate(flops=2**30, bytes_accessed=2**24, transcendentals=0),
        name="panels",
    )(matrix)


def update_kernel(w_ref, r_high, r_low, c_high, c_low, out_ref):
    i = pl.program_id(0)
    prow, pcol = lax.axis_index("prow"), lax.axis_index("pcol")
    row_block = i * 8 + prow
    block = pl.ds(pl.multiple_of(i * NB, NB), NB)
    out_ref[...] = w_ref[block, :] - three(r_high[block, :], r_low[block, :], c_high[...], c_low[...])

    @pl.when(row_block < 2)
    def _():
        out_ref[...] = jnp.zeros((NB, COLS), F32)

    down = lax.broadcasted_iota(jnp.int32, (NB, NB), 0)
    right = lax.broadcasted_iota(jnp.int32, (NB, NB), 1)
    for k in range(2):
        @pl.when(jnp.logical_and(pcol == k, row_block >= k))
        def _(k=k):
            panel = pl.ds(k * NB, NB)
            value = r_high[block, panel].astype(F32) + r_low[block, panel].astype(F32)
            keep = jnp.logical_or(row_block > k, right <= down)
            out_ref[:, 0:NB] = jnp.where(keep, value, 0.0)


def update(matrix, *panels):
    vmem = pl.BlockSpec(memory_space=pltpu.VMEM)
    return pl.pallas_call(
        update_kernel,
        out_shape=jax.ShapeDtypeStruct((ROWS, COLS), F32),
        grid=(ROWS // NB,),
        in_specs=[vmem] * 5,
        out_specs=pl.BlockSpec((NB, COLS), lambda i: (i, 0)),
        compiler_params=pltpu.CompilerParams(vmem_limit_bytes=32 * 2**20),
        cost_estimate=pl.CostEstimate(
            flops=2 * 3 * ROWS * COLS * 2 * NB, bytes_accessed=2**24, transcendentals=0
        ),
        name="update",
    )(matrix, *panels)


def body(matrix):
    return update(*make_panels(matrix))


def solution(mesh):
    spec = P("prow", "pcol")
    return jax.shard_map(body, mesh=mesh, in_specs=(spec,), out_specs=spec, check_vma=False)
```
